128 devices in a mesh: fs: 4 (over y), cp: 4 (over z), ul: 8 (over x, core).
Axes of the slice: x: 4, y: 4, z: 4, core: 2. Of those that a mesh axis runs over, the one named last changes fastest.
Arguments:
- tokens: bfloat16 [16384, 1024], P(('fs', 'cp', 'ul')), may hold values from -6 to 6
- norm_in: float32 [1024], replicated, may hold values from 0.5 to 1.5
- norm_mid: float32 [1024], replicated, may hold values from 0.5 to 1.5
- mamba_gain: float32 [1536], replicated, may hold values from 0.5 to 1.5
- conv_weight: float32 [4, 1792], replicated, may hold values from -3 to 3
- decay_log: float32 [24], replicated, may hold values from -7 to 0.5
- dt_bias: float32 [24], replicated, may hold values from -4 to -1
- skip_gain: float32 [24], replicated, may hold values from 0.5 to 2
- w_in: bfloat16 [1024, 4120], P('fs'), may hold values from -0.1875 to 0.1875
- w_mout: bfloat16 [1536, 1024], P('fs'), may hold values from -0.15625 to 0.15625
- w_aout: bfloat16 [512, 1024], P('fs'), may hold values from -2 to 2
- w_gu: bfloat16 [1024, 4096], P('fs'), may hold values from -0.1875 to 0.1875
- w_down: bfloat16 [2048, 1024], P('fs'), may hold values from -0.125 to 0.125
- grad_out: bfloat16 [16384, 1024], P(('fs', 'cp', 'ul')), may hold values from -6 to 6
Outputs:
- layer_out: bfloat16 [16384, 1024], P(('fs', 'cp', 'ul'))
- grad_tokens: float32 [16384, 1024], P(('fs', 'cp', 'ul'))
- grad_norm_in: float32 [1024], replicated
- grad_norm_mid: float32 [1024], replicated
- grad_mamba_gain: float32 [1536], replicated
- grad_conv_weight: float32 [4, 1792], replicated
- grad_decay_log: float32 [24], replicated
- grad_dt_bias: float32 [24], replicated
- grad_skip_gain: float32 [24], replicated
- grad_w_in: float32 [1024, 4120], P(('fs', 'cp', 'ul'))
- grad_w_mout: float32 [1536, 1024], P(('fs', 'cp', 'ul'))
- grad_w_aout: float32 [512, 1024], P(('fs', 'cp', 'ul'))
- grad_w_gu: float32 [1024, 4096], P(('fs', 'cp', 'ul'))
- grad_w_down: float32 [2048, 1024], P(('fs', 'cp', 'ul'))
The draws below stay inside these ranges and needn't reach their ends.
All inputs are finite; a program needn't handle non-finite values.
Results may differ from the reference program's by a relative error of at most 0.019.
Values may be sent and summed in bfloat16 or wider, within the bound.
A program may use at most 256 MiB of HBM per device.

```python
import jax
import jax.numpy as jnp
import numpy as np
from jax import lax

D = 1024
HM = 24
HP = 64
NS = 128
KW = 4
QUERY_HEAD_TOTAL = 8
KEY_VALUE_HEADS = 2
HEAD_DIMENSION = 64
FF = 2048
SBLK = 256
ABLK = 512
SEQUENCE_TOKENS = 4096
TOKENS = 16384
DS = 1536
CONV = 1792
PROJ = 4120
N_FS = 4
N_UL = 8


def block_scale(own_key, extent, shards, low, high):
    level, own = 1.0, jax.random.fold_in(own_key, 6)
    for axis_at, shards_of in shards:
        draws = jnp.exp(jax.random.uniform(jax.random.fold_in(own, axis_at), (shards_of,), jnp.float32, low / len(shards), high / len(shards)))
        level = level * jnp.repeat(draws, extent[axis_at] // shards_of).reshape([-1 if axis == axis_at else 1 for axis in range(len(extent))])
    return level


def scatter_about(own_key, extent, deviation, bound, shards=(), kind=jnp.bfloat16):
    values = deviation * jax.random.normal(own_key, extent, jnp.float32)
    if shards:
        values = values * block_scale(own_key, extent, shards, -0.22, 0.18)
    return jnp.clip(values, -bound, bound).astype(kind)


def setup_inputs(seed: int = 0) -> dict:
    key_of = jax.random.split(jax.random.key(seed), 15)
    return {
        "tokens": scatter_about(key_of[0], (TOKENS, D), 1.0, 6.0, ((0, 128),)),
        "norm_in": jnp.clip(1.0 + 0.1 * jax.random.normal(key_of[1], (D,), jnp.float32), 0.5, 1.5),
        "norm_mid": jnp.clip(1.0 + 0.1 * jax.random.normal(key_of[2], (D,), jnp.float32), 0.5, 1.5),
        "mamba_gain": jnp.clip(1.0 + 0.1 * jax.random.normal(key_of[3], (DS,), jnp.float32), 0.5, 1.5),
        "conv_weight": scatter_about(key_of[4], (KW, CONV), KW ** -0.5, 3.0, (), jnp.float32),
        "decay_log": jnp.clip(jax.random.uniform(key_of[5], (HM,), jnp.float32, -7.0, 0.5), -7.0, 0.5),
        "dt_bias": jnp.clip(jax.random.uniform(key_of[6], (HM,), jnp.float32, -4.0, -1.0), -4.0, -1.0),
        "skip_gain": jnp.clip(jax.random.uniform(key_of[7], (HM,), jnp.float32, 0.5, 2.0), 0.5, 2.0),
        "w_in": scatter_about(key_of[8], (D, PROJ), D ** -0.5, 0.1875, ((0, 4),)),
        "w_mout": scatter_about(key_of[9], (DS, D), DS ** -0.5, 0.15625, ((0, 4),)),
        "w_aout": scatter_about(key_of[10], (QUERY_HEAD_TOTAL * HEAD_DIMENSION, D), 8 ** -0.5, 2.0, ((0, 4),)),
        "w_gu": scatter_about(key_of[11], (D, 2 * FF), D ** -0.5, 0.1875, ((0, 4),)),
        "w_down": scatter_about(key_of[12], (FF, D), FF ** -0.5, 0.125, ((0, 4),)),
        "grad_out": scatter_about(key_of[13], (TOKENS, D), 1.0, 6.0, ((0, 128),)),
    }


EPSILON = 1e-05
HIGHEST = lax.Precision.HIGHEST
MASKED = -1e+30

@jax.custom_vjp
def low(v):
    return lax.optimization_barrier(v.astype(jnp.bfloat16)).astype(jnp.float32)

@jax.custom_vjp
def reduced_backward(v):
    return v

def low_keep(v):
    return (low(v), None)

def low_pass(kept, grad):
    return (grad,)

def back_keep(v):
    return (v, None)

def back_low(kept, grad):
    return (low(grad),)
low.defvjp(low_keep, low_pass)
reduced_backward.defvjp(back_keep, back_low)

def rms_norm(values, norm_gain):
    return values * lax.rsqrt(lax.optimization_barrier(jnp.mean(values * values, axis=-1, keepdims=True)) + EPSILON) * norm_gain

def matmul_high(left, right):
    return jnp.dot(left, right, precision=HIGHEST)

def causal_conv(values, weights):
    length = values.shape[0]
    extended = jnp.concatenate([jnp.zeros((KW - 1,) + values.shape[1:], values.dtype), values], axis=0)
    running = extended[0:length] * weights[0]
    for offset in range(1, KW):
        running = running + extended[offset:offset + length] * weights[offset]
    return running

def state_space(x_heads, b_heads, c_heads, step_size, log_decay, skip_gain):
    length = step_size.shape[0]
    blocks = length // SBLK
    lower_mask = jnp.tril(jnp.ones((SBLK, SBLK), dtype=bool))

    def one_block(state_now, pieces):
        x_blk, b_blk, c_blk, step_blk, log_blk = pieces
        cumulative = jnp.cumsum(log_blk, axis=0)
        decay_grid = jnp.exp(jnp.where(lower_mask[:, :, None], cumulative[:, None, :] - cumulative[None, :, :], MASKED))
        inner_prod = jnp.einsum('thn,shn->tsh', c_blk, b_blk, precision=HIGHEST)
        within = jnp.einsum('tsh,shp->thp', inner_prod * decay_grid * step_blk[None, :, :], x_blk, precision=HIGHEST)
        carried = jnp.einsum('thn,hpn->thp', c_blk, state_now, precision=HIGHEST) * jnp.exp(cumulative)[:, :, None]
        tail_weight = jnp.exp(cumulative[-1:] - cumulative) * step_blk
        updated = state_now * jnp.exp(cumulative[-1])[:, None, None] + jnp.einsum('sh,shp,shn->hpn', tail_weight, x_blk, b_blk, precision=HIGHEST)
        return (updated, within + carried)
    pieces = (x_heads.reshape(blocks, SBLK, HM, HP), b_heads.reshape(blocks, SBLK, HM, NS), c_heads.reshape(blocks, SBLK, HM, NS), step_size.reshape(blocks, SBLK, HM), log_decay.reshape(blocks, SBLK, HM))
    initial = jnp.zeros((HM, HP, NS), jnp.float32)
    outputs = lax.scan(jax.checkpoint(one_block), initial, pieces)[1]
    return outputs.reshape(length, HM, HP) + skip_gain[None, :, None] * x_heads

def attention(queries, keys, values):
    logit_scale = HEAD_DIMENSION ** (-0.5)
    key_pos = jnp.arange(SEQUENCE_TOKENS, dtype=jnp.int32)

    def one_block(pieces):
        q_blk, block_start = pieces
        raw_scores = reduced_backward(jnp.einsum('qhd,khd->hqk', q_blk, keys, precision=HIGHEST) * logit_scale)
        query_pos = block_start + jnp.arange(ABLK, dtype=jnp.int32)
        visible = query_pos[:, None] >= key_pos[None, :]
        probability_block = low(jax.nn.softmax(jnp.where(visible[None], raw_scores, MASKED), axis=-1))
        return jnp.einsum('hqk,khd->qhd', probability_block, values, precision=HIGHEST)
    blocks = SEQUENCE_TOKENS // ABLK
    starts = jnp.arange(blocks, dtype=jnp.int32) * ABLK
    outputs = lax.map(jax.checkpoint(one_block), (queries.reshape(blocks, ABLK, QUERY_HEAD_TOTAL, HEAD_DIMENSION), starts))
    return outputs.reshape(SEQUENCE_TOKENS, QUERY_HEAD_TOTAL, HEAD_DIMENSION)

def layer(resid_in, norm_in, norm_mid, mamba_gain, conv_weight, decay_log, dt_bias, skip_gain, w_in, w_mout, w_aout, w_gu, w_down):
    mamba_local = HM // N_UL
    query_local = QUERY_HEAD_TOTAL // N_UL
    sharing_count = QUERY_HEAD_TOTAL // KEY_VALUE_HEADS
    key_value_resident = max(1, query_local // sharing_count)
    replicate_heads = np.array([rank_id * query_local // sharing_count + slot_id for rank_id in range(N_UL) for slot_id in range(key_value_resident)])
    head_copy = np.array([head_id // query_local * key_value_resident + head_id % query_local // sharing_count for head_id in range(QUERY_HEAD_TOTAL)])
    head_owner = np.arange(HM) // mamba_local
    normed_in = low(rms_norm(resid_in, norm_in))
    projected = matmul_high(normed_in, w_in)
    gate_pre = reduced_backward(projected[:, :DS])
    x_pre = reduced_backward(low(projected[:, DS:2 * DS]))
    bc_pre = reduced_backward(low(projected[:, 2 * DS:2 * DS + 2 * NS]))
    dt_start = 2 * DS + 2 * NS
    dt_raw = reduced_backward(low(projected[:, dt_start:dt_start + HM]))
    query_begin = dt_start + HM
    q_pre = reduced_backward(low(projected[:, query_begin:query_begin + QUERY_HEAD_TOTAL * HEAD_DIMENSION]))
    key_value_prior = reduced_backward(low(projected[:, query_begin + QUERY_HEAD_TOTAL * HEAD_DIMENSION:]))
    bc_copies = reduced_backward(jnp.broadcast_to(bc_pre[:, None, :], (SEQUENCE_TOKENS, N_UL, 2 * NS)))
    key_value_replicas = reduced_backward(key_value_prior.reshape(SEQUENCE_TOKENS, 2, KEY_VALUE_HEADS, HEAD_DIMENSION)[:, :, replicate_heads])
    x_conv = jax.nn.silu(causal_conv(x_pre, conv_weight[:, :DS]))
    bc_conv = jax.nn.silu(causal_conv(bc_copies, conv_weight[:, DS:]))
    step_size = jax.nn.softplus(dt_raw + dt_bias)
    log_decay = -jnp.exp(decay_log) * step_size
    mixed = state_space(x_conv.reshape(SEQUENCE_TOKENS, HM, HP), bc_conv[:, head_owner, :NS], bc_conv[:, head_owner, NS:], step_size, log_decay, skip_gain)
    mixed = reduced_backward(low(mixed.reshape(SEQUENCE_TOKENS, DS)))
    branch_in = low(rms_norm(mixed * jax.nn.silu(gate_pre), mamba_gain))
    key_heads = key_value_replicas[:, 0][:, head_copy]
    value_heads = key_value_replicas[:, 1][:, head_copy]
    attended = attention(q_pre.reshape(SEQUENCE_TOKENS, QUERY_HEAD_TOTAL, HEAD_DIMENSION), key_heads, value_heads)
    attended = reduced_backward(low(attended.reshape(SEQUENCE_TOKENS, QUERY_HEAD_TOTAL * HEAD_DIMENSION)))
    resid_mid = resid_in + reduced_backward(matmul_high(branch_in, w_mout)) + reduced_backward(matmul_high(attended, w_aout))
    normed_mid = low(rms_norm(resid_mid, norm_mid))
    gate_up = reduced_backward(matmul_high(normed_mid, w_gu))
    hidden = low(jax.nn.silu(gate_up[:, :FF]) * gate_up[:, FF:])
    return resid_mid + reduced_backward(matmul_high(hidden, w_down))

def reference(tokens, norm_in, norm_mid, mamba_gain, conv_weight, decay_log, dt_bias, skip_gain, w_in, w_mout, w_aout, w_gu, w_down, grad_out):
    sequences = tokens.astype(jnp.float32).reshape(N_FS, SEQUENCE_TOKENS, D)
    matrices = (w_in.astype(jnp.float32), w_mout.astype(jnp.float32), w_aout.astype(jnp.float32), w_gu.astype(jnp.float32), w_down.astype(jnp.float32))

    def whole(all_seqs, gain_in, gain_mid, gain_mamba, conv_taps, decay_rates, bias_step, skip_terms, mat_in, mat_mout, mat_aout, mat_gu, mat_down):

        def one_sequence(one_seq):
            return layer(one_seq, gain_in, gain_mid, gain_mamba, conv_taps, decay_rates, bias_step, skip_terms, mat_in, mat_mout, mat_aout, mat_gu, mat_down)
        return lax.map(one_sequence, all_seqs)
    layer_out, pull_back = jax.vjp(whole, sequences, norm_in, norm_mid, mamba_gain, conv_weight, decay_log, dt_bias, skip_gain, matrices[0], matrices[1], matrices[2], matrices[3], matrices[4])
    grads = pull_back(grad_out.astype(jnp.float32).reshape(N_FS, SEQUENCE_TOKENS, D))
    return (layer_out.reshape(TOKENS, D).astype(jnp.bfloat16), grads[0].reshape(TOKENS, D), grads[1], grads[2], grads[3], grads[4], grads[5], grads[6], grads[7], grads[8], grads[9], grads[10], grads[11], grads[12])
```

```python
import functools
import jax
import jax.numpy as jnp
from jax import lax
from jax.experimental import pallas as pl
from jax.experimental.pallas import tpu as pltpu
from jax.sharding import Mesh
from jax.sharding import PartitionSpec as P

HP = 64
NS = 128
KW = 4
SBLK = 256
MASKED = -1e30
HIGHEST = lax.Precision.HIGHEST
F32 = jnp.float32
BF16 = jnp.bfloat16
VMEM_LIMIT = 56 * 1024 * 1024
XW = 192
CW = 448
HALO = 16
DT_AT = 640
Q_AT = 448
KV_AT = 512


def nn(a, b, precision=None):
    return lax.dot_general(
        a, b, (((1,), (0,)), ((), ())), precision=precision, preferred_element_type=F32
    )


def nt(a, b):
    return lax.dot_general(a, b, (((1,), (1,)), ((), ())), preferred_element_type=F32)


def tn(a, b):
    return lax.dot_general(a, b, (((0,), (0,)), ((), ())), preferred_element_type=F32)


def iota(shape, dim):
    return lax.broadcasted_iota(jnp.int32, shape, dim)


def spread(per_head, rows):
    return jnp.concatenate(
        [jnp.broadcast_to(per_head[:, h : h + 1], (rows, HP)) for h in range(XW // HP)], axis=1
    )


def head_sum_matrix():
    return (iota((XW, 128), 0) // HP == iota((XW, 128), 1)).astype(F32)


def conv_pre(ext, weights, base, lanes=slice(None)):
    pre = ext[pl.ds(base + HALO - 3, SBLK), :] * weights[0:1, :]
    for k in range(1, KW):
        pre = pre + ext[pl.ds(base + HALO - 3 + k, SBLK), :] * weights[k : k + 1, :]
    return pre


def step_and_log(slab, par_ref, base):
    raw = slab[pl.ds(base, SBLK), DT_AT:].astype(F32) + par_ref[1:2, :]
    step = jnp.maximum(raw, 0.0) + jnp.log1p(jnp.exp(-jnp.abs(raw)))
    return raw, step, -jnp.exp(par_ref[0:1, :]) * step


def ssd_forward(slab, halo, taps, par, y_out, state_out, c_out, cum_out, entry_out, ext):
    length = slab.shape[0]
    ext[pl.ds(0, HALO), :] = halo[...].astype(F32)
    ext[pl.ds(HALO, length), :] = slab[:, :CW].astype(F32)
    weights = taps[...]
    lower = iota((SBLK, SBLK), 0) >= iota((SBLK, SBLK), 1)
    tri = lower.astype(F32)
    state_out[...] = jnp.zeros_like(state_out)
    before = jnp.zeros((1, 128), F32)
    for k in range(length // SBLK):
        base = k * SBLK
        pre = conv_pre(ext, weights, base)
        conv = pre * jax.nn.sigmoid(pre)
        b_low = conv[:, :NS].astype(BF16)
        c_low = conv[:, NS : 2 * NS].astype(BF16)
        x = conv[:, 2 * NS :]
        raw, step, log = step_and_log(slab, par, base)
        cum = nn(tri, log, HIGHEST)
        cum_t = cum.T
        u = x * spread(step, SBLK)
        u_low = u.astype(BF16)
        inner = nt(c_low, b_low)
        state = state_out[pl.ds(0, XW), :]
        entry_out[k] = state
        parts = []
        for h in range(XW // HP):
            decay = jnp.exp(
                jnp.where(lower, cum[:, h : h + 1] - cum_t[h : h + 1, :], MASKED)
            )
            parts.append(nn((inner * decay).astype(BF16), u_low[:, h * HP : (h + 1) * HP]))
        carried = nt(c_low, state.astype(BF16)) * spread(jnp.exp(cum), SBLK)
        y_out[pl.ds(base, SBLK), :] = (
            jnp.concatenate(parts, axis=1) + carried + spread(par[2:3, :], 1) * x
        )
        last = cum[SBLK - 1 : SBLK, :]
        tail = (u * spread(jnp.exp(last - cum), SBLK)).astype(BF16)
        shrink = jnp.concatenate(
            [
                jnp.broadcast_to(jnp.exp(last[:, h : h + 1]), (HP, NS))
                for h in range(XW // HP)
            ],
            axis=0,
        )
        state_out[pl.ds(0, XW), :] = state * shrink + tn(tail, b_low)
        c_out[pl.ds(base, SBLK), :] = c_low
        cum_out[pl.ds(base, SBLK), :] = cum + before
        before = before + last
    state_out[pl.ds(XW, 8), :] = jnp.broadcast_to(before, (8, 128))


def ssd_forward_call(slab, halo, taps, par):
    length = slab.shape[0]
    return pl.pallas_call(
        ssd_forward,
        out_shape=(
            jax.ShapeDtypeStruct((length, XW), F32),
            jax.ShapeDtypeStruct((XW + 8, NS), F32),
            jax.ShapeDtypeStruct((length, NS), BF16),
            jax.ShapeDtypeStruct((length, 128), F32),
            jax.ShapeDtypeStruct((length // SBLK, XW, NS), F32),
        ),
        scratch_shapes=[pltpu.VMEM((length + HALO, CW), F32)],
        compiler_params=pltpu.CompilerParams(vmem_limit_bytes=VMEM_LIMIT),
        cost_estimate=pl.CostEstimate(
            flops=8_000_000_000, bytes_accessed=8_000_000, transcendentals=1_000_000
        ),
        name="ssd_forward",
    )(slab, halo, taps, par)


def shrink_rows(log_row):
    return jnp.concatenate(
        [jnp.broadcast_to(jnp.exp(log_row[:, h : h + 1]), (HP, NS)) for h in range(XW // HP)],
        axis=0,
    )


def ssd_join(y, c, cum, near, mid, far, attended, out, entering):
    state = near[pl.ds(0, XW), :] + shrink_rows(near[XW : XW + 1, :]) * (
        mid[pl.ds(0, XW), :] + shrink_rows(mid[XW : XW + 1, :]) * far[pl.ds(0, XW), :]
    )
    entering[...] = state
    state_low = state.astype(BF16)
    rows = y.shape[0]
    for base in range(0, rows, SBLK):
        at = pl.ds(base, SBLK)
        mixed = y[at, :] + nt(c[at, :], state_low) * spread(jnp.exp(cum[at, :]), SBLK)
        out[at, :] = jnp.concatenate([mixed, attended[at, :]], axis=1).astype(BF16)


def ssd_join_call(y, c, cum, near, mid, far, attended):
    return pl.pallas_call(
        ssd_join,
        out_shape=(
            jax.ShapeDtypeStruct((y.shape[0], XW + HP), BF16),
            jax.ShapeDtypeStruct((XW, NS), F32),
        ),
        compiler_params=pltpu.CompilerParams(vmem_limit_bytes=VMEM_LIMIT),
        name="ssd_join",
    )(y, c, cum, near, mid, far, attended)


def ssd_entry_gradient(grad, c, cum, out):
    rows = grad.shape[0]
    total = jnp.zeros((XW, NS), F32)
    for base in range(0, rows, SBLK):
        at = pl.ds(base, SBLK)
        scaled = grad[at, :XW].astype(F32) * spread(jnp.exp(cum[at, :]), SBLK)
        total = total + tn(scaled.astype(BF16), c[at, :])
    out[pl.ds(0, XW), :] = total
    out[pl.ds(XW, 8), :] = jnp.broadcast_to(cum[rows - 1 : rows, :], (8, 128))


def ssd_entry_gradient_call(grad, c, cum):
    return pl.pallas_call(
        ssd_entry_gradient,
        out_shape=jax.ShapeDtypeStruct((XW + 8, NS), F32),
        compiler_params=pltpu.CompilerParams(vmem_limit_bytes=VMEM_LIMIT),
        name="ssd_entry_gradient",
    )(grad, c, cum)


def ssd_backward(
    slab, halo, taps, par, grad, entry, cum_all, entering, near, mid, far,
    grad_in, grad_dt, grad_rim, grad_taps, grad_par, ext, gpre,
):
    length = slab.shape[0]
    chunks = length // SBLK
    ext[pl.ds(0, HALO), :] = halo[...].astype(F32)
    ext[pl.ds(HALO, length), :] = slab[:, :CW].astype(F32)
    gpre[pl.ds(length, HALO), :] = jnp.zeros((HALO, CW), F32)
    weights = taps[...]
    lower = iota((SBLK, SBLK), 0) >= iota((SBLK, SBLK), 1)
    tri = lower.astype(F32)
    upper = (iota((SBLK, SBLK), 0) <= iota((SBLK, SBLK), 1)).astype(F32)
    hsum = head_sum_matrix()
    rate = jnp.exp(par[0:1, :])
    skip = spread(par[2:3, :], 1)
    enter = entering[...]
    later = near[pl.ds(0, XW), :] + shrink_rows(near[XW : XW + 1, :]) * (
        mid[pl.ds(0, XW), :] + shrink_rows(mid[XW : XW + 1, :]) * far[pl.ds(0, XW), :]
    )
    g_decay = jnp.zeros((1, 128), F32)
    g_bias = jnp.zeros((1, 128), F32)
    g_skip = jnp.zeros((1, 128), F32)
    for k in reversed(range(chunks)):
        base = k * SBLK
        at = pl.ds(base, SBLK)
        pre = conv_pre(ext, weights, base)
        sig = jax.nn.sigmoid(pre)
        conv = pre * sig
        b_low = conv[:, :NS].astype(BF16)
        c_low = conv[:, NS : 2 * NS].astype(BF16)
        x = conv[:, 2 * NS :]
        raw, step, log = step_and_log(slab, par, base)
        cum = nn(tri, log, HIGHEST)
        cum_t = cum.T
        last = cum[SBLK - 1 : SBLK, :]
        step_wide = spread(step, SBLK)
        u_low = (x * step_wide).astype(BF16)
        u = u_low.astype(F32)
        gy_low = grad[at, :XW]
        gy = gy_low.astype(F32)
        if k:
            state = entry[k] + shrink_rows(cum_all[base - 1 : base, :]) * enter
        else:
            state = enter
        state_low = state.astype(BF16)
        later_low = later.astype(BF16)
        inner = nt(c_low, b_low)
        g_inner = jnp.zeros((SBLK, SBLK), F32)
        y_parts, gu_parts = [], []
        for h in range(XW // HP):
            lanes = slice(h * HP, (h + 1) * HP)
            decay = jnp.exp(
                jnp.where(lower, cum[:, h : h + 1] - cum_t[h : h + 1, :], MASKED)
            )
            kernel = (inner * decay).astype(BF16)
            y_parts.append(nn(kernel, u_low[:, lanes]))
            gu_parts.append(tn(kernel, gy_low[:, lanes]))
            g_inner = g_inner + nt(gy_low[:, lanes], u_low[:, lanes]) * decay
        g_inner_low = g_inner.astype(BF16)
        enter_wide = spread(jnp.exp(cum), SBLK)
        tail_wide = spread(jnp.exp(last - cum), SBLK)
        gy_scaled = (gy * enter_wide).astype(BF16)
        u_scaled = (u * tail_wide).astype(BF16)
        y = jnp.concatenate(y_parts, axis=1) + nt(c_low, state_low) * enter_wide
        tail = nt(b_low, later_low) * tail_wide
        gu = jnp.concatenate(gu_parts, axis=1) + tail
        gc = nn(g_inner_low, b_low) + nn(gy_scaled, state_low)
        gb = tn(g_inner_low, c_low) + nn(u_scaled, later_low)
        shrink = shrink_rows(last)
        both = nn(gy * y - u * gu, hsum, HIGHEST)
        tail_sum = jnp.sum(nn(u * tail, hsum, HIGHEST), axis=0, keepdims=True)
        across = jnp.sum(
            jnp.sum(later * state * shrink, axis=1, keepdims=True) * hsum, axis=0, keepdims=True
        )
        g_log = nn(upper, both, HIGHEST) + tail_sum + across
        g_step = nn(x * gu, hsum, HIGHEST) - rate * g_log
        g_raw = g_step * jax.nn.sigmoid(raw)
        g_decay = g_decay + jnp.sum(g_log * log, axis=0, keepdims=True)
        g_bias = g_bias + jnp.sum(g_raw, axis=0, keepdims=True)
        g_skip = g_skip + jnp.sum(nn(gy * x, hsum, HIGHEST), axis=0, keepdims=True)
        grad_dt[at, :] = g_raw
        g_conv = jnp.concatenate([gb, gc, step_wide * gu + skip * gy], axis=1)
        gpre[at, :] = g_conv * (sig + conv * (1.0 - sig))
        later = shrink * later + tn(gy_scaled, c_low)
    for k in range(chunks):
        base = k * SBLK
        acc = gpre[pl.ds(base + 3, SBLK), :] * weights[0:1, :]
        for tap in range(1, KW):
            acc = acc + gpre[pl.ds(base + 3 - tap, SBLK), :] * weights[tap : tap + 1, :]
        grad_in[pl.ds(base, SBLK), :] = acc
    first = gpre[pl.ds(0, 8), :]
    rim = jnp.zeros((8, CW), F32)
    rows = iota((8, CW), 0)
    for back in range(1, KW):
        term = jnp.zeros((1, CW), F32)
        for tap in range(KW):
            t = 3 - tap - back
            if 0 <= t:
                term = term + first[t : t + 1, :] * weights[tap : tap + 1, :]
        rim = jnp.where(rows == 8 - back, term, rim)
    grad_rim[...] = rim
    g_taps = jnp.zeros((8, CW), F32)
    rows = iota((8, CW), 0)
    for tap in range(KW):
        total = jnp.zeros((1, CW), F32)
        for k in range(chunks):
            base = k * SBLK
            total = total + jnp.sum(
                gpre[pl.ds(base, SBLK), :] * ext[pl.ds(base + HALO - 3 + tap, SBLK), :],
                axis=0,
                keepdims=True,
            )
        g_taps = jnp.where(rows == tap, total, g_taps)
    grad_taps[...] = g_taps
    rows = iota((8, 128), 0)
    grad_par[...] = jnp.where(
        rows == 0, g_decay, jnp.where(rows == 1, g_bias, jnp.where(rows == 2, g_skip, 0.0))
    )


def ssd_backward_call(slab, halo, taps, par, grad, entry, cum, entering, near, mid, far):
    length = slab.shape[0]
    return pl.pallas_call(
        ssd_backward,
        out_shape=(
            jax.ShapeDtypeStruct((length, CW), F32),
            jax.ShapeDtypeStruct((length, 128), F32),
            jax.ShapeDtypeStruct((8, CW), F32),
            jax.ShapeDtypeStruct((8, CW), F32),
            jax.ShapeDtypeStruct((8, 128), F32),
        ),
        scratch_shapes=[
            pltpu.VMEM((length + HALO, CW), F32),
            pltpu.VMEM((length + HALO, CW), F32),
        ],
        compiler_params=pltpu.CompilerParams(vmem_limit_bytes=VMEM_LIMIT),
        cost_estimate=pl.CostEstimate(
            flops=20_000_000_000, bytes_accessed=12_000_000, transcendentals=2_000_000
        ),
        name="ssd_backward",
    )(slab, halo, taps, par, grad, entry, cum, entering, near, mid, far)


QB = 256
KB = 512


def place_keys(rank, parts, kv):
    length = parts[0].shape[0]
    for back, part in enumerate(parts):

        @pl.when(rank >= back)
        def _():
            kv[pl.ds(pl.multiple_of((rank - back) * length, length), length), :] = part[...]


def attend_forward(rank_ref, slab, near, mid, far, out, lse, kv, own):
    length = slab.shape[0]
    rank = rank_ref[0]
    offset = rank * length
    scale = HP**-0.5
    ahead = iota((QB, KB), 0) - iota((QB, KB), 1)
    own[...] = slab[:, KV_AT:DT_AT]
    place_keys(rank, (own, near, mid, far), kv)

    def q_step(i, _):
        at = pl.ds(pl.multiple_of(i * QB, QB), QB)
        q_blk = (slab[at, Q_AT:KV_AT].astype(F32) * scale).astype(BF16)
        first = offset + i * QB

        def block(j, carry, masked):
            top, total, acc = carry
            at = pl.ds(pl.multiple_of(j * KB, KB), KB)
            s = nt(q_blk, kv[at, :HP])
            if masked:
                s = jnp.where(ahead >= j * KB - first, s, MASKED)
            new = jnp.maximum(top, jnp.max(s, axis=1, keepdims=True))
            p = jnp.exp(s - new)
            fade = jnp.exp(top - new)
            total = total * fade + jnp.sum(p, axis=1, keepdims=True)
            acc = acc * fade + nn(p.astype(BF16), kv[at, HP:])
            return new, total, acc

        whole = first // KB
        carry = (
            jnp.full((QB, 1), MASKED, F32),
            jnp.zeros((QB, 1), F32),
            jnp.zeros((QB, HP), F32),
        )
        carry = lax.fori_loop(0, whole, lambda j, c: block(j, c, False), carry)
        top, total, acc = block(whole, carry, True)
        out[at, :] = acc / total
        lse[at, :] = jnp.broadcast_to(top + jnp.log(total), (QB, 128))
        return 0

    lax.fori_loop(0, length // QB, q_step, 0)


def attend_forward_call(rank, slab, near, mid, far):
    length = slab.shape[0]
    vm = pl.BlockSpec(memory_space=pltpu.VMEM)
    return pl.pallas_call(
        attend_forward,
        in_specs=[pl.BlockSpec(memory_space=pltpu.SMEM)] + [vm] * 4,
        out_shape=(
            jax.ShapeDtypeStruct((length, HP), F32),
            jax.ShapeDtypeStruct((length, 128), F32),
        ),
        scratch_shapes=[
            pltpu.VMEM((4 * length, 2 * HP), BF16),
            pltpu.VMEM((length, 2 * HP), BF16),
        ],
        compiler_params=pltpu.CompilerParams(vmem_limit_bytes=VMEM_LIMIT),
        cost_estimate=pl.CostEstimate(
            flops=8_000_000_000, bytes_accessed=4_000_000, transcendentals=4_000_000
        ),
        name="attend_forward",
    )(rank, slab, near, mid, far)


def attend_backward(
    rank_ref, slab, near, mid, far, g, out, lse, gq, g_own, g_near, g_mid, g_far, kv, own, acc
):
    length = slab.shape[0]
    rank = rank_ref[0]
    offset = rank * length
    scale = HP**-0.5
    ahead = iota((QB, KB), 0) - iota((QB, KB), 1)
    own[...] = slab[:, KV_AT:DT_AT]
    place_keys(rank, (own, near, mid, far), kv)
    acc[...] = jnp.zeros_like(acc)

    def q_step(i, _):
        at_q = pl.ds(pl.multiple_of(i * QB, QB), QB)
        q_blk = (slab[at_q, Q_AT:KV_AT].astype(F32) * scale).astype(BF16)
        g_low = g[at_q, XW:]
        delta = jnp.sum(g_low.astype(F32) * out[at_q, :], axis=1, keepdims=True)
        log_total = lse[at_q, 0:1]
        first = offset + i * QB

        def block(j, gq_acc, masked):
            at = pl.ds(pl.multiple_of(j * KB, KB), KB)
            k_blk = kv[at, :HP]
            s = nt(q_blk, k_blk)
            if masked:
                s = jnp.where(ahead >= j * KB - first, s, MASKED)
            p = jnp.exp(s - log_total)
            dp = nt(g_low, kv[at, HP:])
            ds = (p * (dp - delta)).astype(BF16)
            acc[at, :] += jnp.concatenate([tn(ds, q_blk), tn(p.astype(BF16), g_low)], axis=1)
            return gq_acc + nn(ds, k_blk)

        whole = first // KB
        carry = jnp.zeros((QB, HP), F32)
        carry = lax.fori_loop(0, whole, lambda j, c: block(j, c, False), carry)
        gq[at_q, :] = block(whole, carry, True) * scale
        return 0

    lax.fori_loop(0, length // QB, q_step, 0)
    for back, target in enumerate((g_own, g_near, g_mid, g_far)):

        @pl.when(rank >= back)
        def _():
            at = pl.ds(pl.multiple_of((rank - back) * length, length), length)
            target[...] = acc[at, :].astype(target.dtype)

        @pl.when(rank < back)
        def _():
            target[...] = jnp.zeros_like(target)


def attend_backward_call(rank, slab, near, mid, far, g, out, lse):
    length = slab.shape[0]
    vm = pl.BlockSpec(memory_space=pltpu.VMEM)
    keys = jax.ShapeDtypeStruct((length, 2 * HP), BF16)
    return pl.pallas_call(
        attend_backward,
        in_specs=[pl.BlockSpec(memory_space=pltpu.SMEM)] + [vm] * 7,
        out_shape=(
            jax.ShapeDtypeStruct((length, HP), F32),
            jax.ShapeDtypeStruct((length, 2 * HP), F32),
            keys,
            keys,
            keys,
        ),
        scratch_shapes=[
            pltpu.VMEM((4 * length, 2 * HP), BF16),
            pltpu.VMEM((length, 2 * HP), BF16),
            pltpu.VMEM((4 * length, 2 * HP), F32),
        ],
        compiler_params=pltpu.CompilerParams(vmem_limit_bytes=VMEM_LIMIT),
        cost_estimate=pl.CostEstimate(
            flops=20_000_000_000, bytes_accessed=4_000_000, transcendentals=4_000_000
        ),
        name="attend_backward",
    )(rank, slab, near, mid, far, g, out, lse)


HM = 24
GROUPS = 8
HEADS = 8
KEY_HEADS = 2
FF = 2048
DS = 1536
PROJ = 4120
PROJ_WIDE = 4352
EPSILON = 1e-05
TOKEN_AXES = ("fs", "cp", "ux", "uc")


def rms_norm(values, norm_gain):
    return (
        values * lax.rsqrt(jnp.mean(values * values, axis=-1, keepdims=True) + EPSILON) * norm_gain
    )


def gated_norm(mixed_heads, gate_pre, norm_gain):
    return rms_norm(mixed_heads * jax.nn.silu(gate_pre), norm_gain)


def from_behind(block, distance):
    return lax.ppermute(block, "cp", [(i - distance, i) for i in range(distance, 4)])


def from_ahead(block, distance):
    return lax.ppermute(block, "cp", [(i, i - distance) for i in range(distance, 4)])


def other_core(block):
    return lax.ppermute(block, "uc", [(0, 1), (1, 0)])


def columns_half(block, half):
    width = block.shape[1] // 2
    return lax.dynamic_slice_in_dim(block, half * width, width, 1)


def weight_gradient(left, right, core):
    lefts = jnp.concatenate([left, other_core(left)], axis=0)
    rights = jnp.concatenate(
        [columns_half(right, core), other_core(columns_half(right, 1 - core))], axis=0
    )
    part = tn(lefts, rights).astype(BF16)
    for axis in ("fs", "cp", "ux"):
        part = lax.psum_scatter(part, axis, scatter_dimension=0, tiled=True)
    rows = part.shape[0] // 2
    mine = lax.dynamic_slice_in_dim(part, core * rows, rows, 0)
    theirs = other_core(lax.dynamic_slice_in_dim(part, (1 - core) * rows, rows, 0))
    return jnp.concatenate(
        [jnp.where(core == 0, mine, theirs), jnp.where(core == 0, theirs, mine)], axis=1
    ).astype(F32)


def shards(
    tokens,
    norm_in,
    norm_mid,
    mamba_gain,
    conv_weight,
    decay_log,
    dt_bias,
    skip_gain,
    w_in,
    w_mout,
    w_aout,
    w_gu,
    w_down,
    grad_out,
):
    part_rank = lax.axis_index("cp")
    core = lax.axis_index("uc")
    group = lax.axis_index("ux") * 2 + core
    rows = tokens.shape[0]
    length = GROUPS * rows
    heads = HM // GROUPS
    full_in, full_mout, full_aout, full_gu, full_down = (
        lax.all_gather(w, "fs", axis=0, tiled=True) for w in (w_in, w_mout, w_aout, w_gu, w_down)
    )

    def to_groups(blocks):
        return lax.all_to_all(blocks, ("ux", "uc"), split_axis=0, concat_axis=0, tiled=True)

    resid_in = tokens.astype(F32)
    normed_f, in_back = jax.vjp(rms_norm, resid_in, norm_in)
    normed_in = normed_f.astype(BF16)
    projected = nn(normed_in, full_in)
    gate_pre = projected[:, :DS]
    low = projected[:, DS:].astype(BF16)
    q_at = DS + 2 * NS + HM
    k_at = q_at + HEADS * HP
    v_at = k_at + KEY_HEADS * HP
    blocks = []
    for g in range(GROUPS):
        key = g * KEY_HEADS // GROUPS
        blocks.append(
            jnp.concatenate(
                [
                    low[:, DS : DS + 2 * NS],
                    low[:, g * XW : (g + 1) * XW],
                    low[:, q_at + g * HP : q_at + (g + 1) * HP],
                    low[:, k_at + key * HP : k_at + (key + 1) * HP],
                    low[:, v_at + key * HP : v_at + (key + 1) * HP],
                    low[:, DS + 2 * NS + g * heads : DS + 2 * NS + (g + 1) * heads],
                    jnp.zeros((rows, 128 - heads), BF16),
                ],
                axis=1,
            )
        )
    slab = to_groups(jnp.stack(blocks)).reshape(length, DT_AT + 128)

    taps = jnp.concatenate(
        [conv_weight[:, DS:], lax.dynamic_slice_in_dim(conv_weight, group * XW, XW, 1)], axis=1
    )
    taps = jnp.pad(taps, ((0, 8 - KW), (0, 0)))
    per_head = jnp.stack([decay_log, dt_bias, skip_gain])
    par = jnp.pad(
        lax.dynamic_slice_in_dim(per_head, group * heads, heads, 1), ((0, 5), (0, 128 - heads))
    )
    rank = part_rank.astype(jnp.int32).reshape(1)

    halo = from_behind(slab[length - HALO :, :CW], 1)
    own_keys = slab[:, KV_AT:DT_AT]
    keys = [from_behind(own_keys, d) for d in (1, 2, 3)]
    y, state, c_low, cum, entry = ssd_forward_call(slab, halo, taps, par)
    states = [from_behind(state, d) for d in (1, 2, 3)]
    attended, lse = attend_forward_call(rank, slab, *keys)
    joined, entering = ssd_join_call(y, c_low, cum, *states, attended)
    tok = to_groups(joined.reshape(GROUPS, rows, XW + HP)).transpose(1, 0, 2)
    mixed_tok = tok[:, :, :XW].reshape(rows, DS)
    attended_tok = tok[:, :, XW:].reshape(rows, HEADS * HP)

    branch_f, gate_back = jax.vjp(gated_norm, mixed_tok.astype(F32), gate_pre, mamba_gain)
    branch_low = branch_f.astype(BF16)
    resid_mid = resid_in + nn(branch_low, full_mout) + nn(attended_tok, full_aout)
    normed_mid_f, mid_back = jax.vjp(rms_norm, resid_mid, norm_mid)
    normed_mid = normed_mid_f.astype(BF16)
    gate_up = nn(normed_mid, full_gu)
    gate_half = gate_up[:, :FF]
    up_half = gate_up[:, FF:]
    sigmoid_gate = jax.nn.sigmoid(gate_half)
    hidden = (gate_half * sigmoid_gate * up_half).astype(BF16)
    layer_out = (resid_mid + nn(hidden, full_down)).astype(BF16)
    grad_hidden = nt(grad_out, full_down)
    grad_gate = grad_hidden * up_half * sigmoid_gate * (1.0 + gate_half * (1.0 - sigmoid_gate))
    grad_up = grad_hidden * gate_half * sigmoid_gate
    grad_gate_up = jnp.concatenate([grad_gate, grad_up], axis=1).astype(BF16)
    resid_back, grad_norm_mid = mid_back(nt(grad_gate_up, full_gu))
    grad_resid = grad_out.astype(F32) + resid_back
    resid_low = grad_resid.astype(BF16)
    grad_mixed, grad_gate_pre, grad_mamba_gain = gate_back(nt(resid_low, full_mout))
    grad_attended = nt(resid_low, full_aout)
    grad_blocks = jnp.concatenate(
        [
            grad_mixed.astype(BF16).reshape(rows, GROUPS, XW),
            grad_attended.astype(BF16).reshape(rows, GROUPS, HP),
        ],
        axis=2,
    ).transpose(1, 0, 2)
    grad = to_groups(grad_blocks).reshape(length, XW + HP)
    grad_down = weight_gradient(hidden, grad_out, core)
    grad_gu = weight_gradient(normed_mid, grad_gate_up, core)
    grad_mout = weight_gradient(branch_low, resid_low, core)
    grad_aout = weight_gradient(attended_tok, resid_low, core)

    entry_gradient = ssd_entry_gradient_call(grad, c_low, cum)
    later = [from_ahead(entry_gradient, d) for d in (1, 2, 3)]
    grad_query, key_own, *key_parts = attend_backward_call(rank, slab, *keys, grad, attended, lse)
    key_parts = [from_ahead(p, d + 1) for d, p in enumerate(key_parts)]
    grad_in_cols, grad_dt, rim, grad_taps, grad_par = ssd_backward_call(
        slab, halo, taps, par, grad, entry, cum, entering, *later
    )
    rim = from_ahead(rim, 1)
    grad_cols = jnp.concatenate(
        [grad_in_cols[: length - 8], grad_in_cols[length - 8 :] + rim], axis=0
    )
    grad_keys = key_own + sum(p.astype(F32) for p in key_parts)
    back = jnp.concatenate(
        [grad_cols.astype(BF16), grad_query.astype(BF16), grad_keys.astype(BF16), grad_dt.astype(BF16)],
        axis=1,
    )
    back = to_groups(back.reshape(GROUPS, rows, DT_AT + 128))
    grad_x = back[:, :, 2 * NS : CW].transpose(1, 0, 2).reshape(rows, DS)
    grad_bc = jnp.sum(back[:, :, : 2 * NS].astype(F32), axis=0).astype(BF16)
    grad_q = back[:, :, Q_AT:KV_AT].transpose(1, 0, 2).reshape(rows, HEADS * HP)
    shared = back[:, :, KV_AT:DT_AT].astype(F32).reshape(KEY_HEADS, GROUPS // KEY_HEADS, rows, 2, HP)
    grad_kv = jnp.sum(shared, axis=1).transpose(1, 2, 0, 3).reshape(rows, 2 * KEY_HEADS * HP)
    grad_dt_tok = back[:, :, DT_AT : DT_AT + heads].transpose(1, 0, 2).reshape(rows, HM)
    grad_proj = jnp.concatenate(
        [
            grad_gate_pre.astype(BF16),
            grad_x,
            grad_bc,
            grad_dt_tok,
            grad_q,
            grad_kv.astype(BF16),
            jnp.zeros((rows, PROJ_WIDE - PROJ), BF16),
        ],
        axis=1,
    )
    grad_in = weight_gradient(normed_in, grad_proj, core)[:, :PROJ]
    tokens_back, grad_norm_in = in_back(nt(grad_proj[:, :PROJ], full_in))
    grad_tokens = grad_resid + tokens_back

    conv_full = jnp.concatenate(
        [
            lax.dynamic_update_slice_in_dim(
                jnp.zeros((KW, DS), F32), grad_taps[:KW, 2 * NS :], group * XW, 1
            ),
            grad_taps[:KW, : 2 * NS],
        ],
        axis=1,
    )
    head_full = lax.dynamic_update_slice_in_dim(
        jnp.zeros((3, HM), F32), grad_par[:3, :heads], group * heads, 1
    )
    small = lax.psum(
        (grad_norm_in, grad_norm_mid, grad_mamba_gain, conv_full, head_full), TOKEN_AXES
    )
    return (
        layer_out,
        grad_tokens,
        small[0],
        small[1],
        small[2],
        small[3],
        small[4][0],
        small[4][1],
        small[4][2],
        grad_in,
        grad_mout,
        grad_aout,
        grad_gu,
        grad_down,
    )


def solution(mesh):
    fine = Mesh(mesh.devices.reshape(4, 4, 4, 2), TOKEN_AXES)
    by_token = P(TOKEN_AXES, None)
    by_row = P("fs", None)
    return jax.shard_map(
        shards,
        mesh=fine,
        in_specs=(by_token,) + (P(),) * 7 + (by_row,) * 5 + (by_token,),
        out_specs=(by_token, by_token) + (P(),) * 7 + (by_token,) * 5,
        check_vma=False,
    )
```

```python
import math

import jax
import jax.numpy as jnp
from jax import lax
from jax.experimental import pallas as pl
from jax.experimental.pallas import tpu as pltpu
from jax.sharding import Mesh
from jax.sharding import PartitionSpec as P

HP = 64
NS = 128
KW = 4
SBLK = 256
MASKED = -1e30
HIGHEST = lax.Precision.HIGHEST
F32 = jnp.float32
BF16 = jnp.bfloat16
VMEM_LIMIT = 56 * 1024 * 1024
XW = 192
CW = 448
HALO = 16
DT_AT = 640
Q_AT = 448
KV_AT = 512


def nn(a, b, precision=None):
    return lax.dot_general(
        a, b, (((1,), (0,)), ((), ())), precision=precision, preferred_element_type=F32
    )


def nt(a, b):
    return lax.dot_general(a, b, (((1,), (1,)), ((), ())), preferred_element_type=F32)


def tn(a, b):
    return lax.dot_general(a, b, (((0,), (0,)), ((), ())), preferred_element_type=F32)


def iota(shape, dim):
    return lax.broadcasted_iota(jnp.int32, shape, dim)


def spread(per_head, rows):
    return jnp.concatenate(
        [jnp.broadcast_to(per_head[:, h : h + 1], (rows, HP)) for h in range(XW // HP)], axis=1
    )


def head_sum_matrix():
    return (iota((XW, 128), 0) // HP == iota((XW, 128), 1)).astype(F32)


def conv_pre(ext, weights, base, lanes=slice(None)):
    pre = ext[pl.ds(base + HALO - 3, SBLK), :] * weights[0:1, :]
    for k in range(1, KW):
        pre = pre + ext[pl.ds(base + HALO - 3 + k, SBLK), :] * weights[k : k + 1, :]
    return pre


def step_and_log(slab, par_ref, base):
    raw = slab[pl.ds(base, SBLK), DT_AT:].astype(F32) + par_ref[1:2, :]
    step = jnp.maximum(raw, 0.0) + jnp.log1p(jnp.exp(-jnp.abs(raw)))
    return raw, step, -jnp.exp(par_ref[0:1, :]) * step


def ssd_forward(slab, halo, taps, par, y_out, state_out, c_out, cum_out, entry_out, ext):
    length = slab.shape[0]
    ext[pl.ds(0, HALO), :] = halo[...].astype(F32)
    ext[pl.ds(HALO, length), :] = slab[:, :CW].astype(F32)
    weights = taps[...]
    lower = iota((SBLK, SBLK), 0) >= iota((SBLK, SBLK), 1)
    tri = lower.astype(F32)
    state_out[...] = jnp.zeros_like(state_out)
    before = jnp.zeros((1, 128), F32)
    for k in range(length // SBLK):
        base = k * SBLK
        pre = conv_pre(ext, weights, base)
        conv = pre * jax.nn.sigmoid(pre)
        b_low = conv[:, :NS].astype(BF16)
        c_low = conv[:, NS : 2 * NS].astype(BF16)
        x = conv[:, 2 * NS :]
        raw, step, log = step_and_log(slab, par, base)
        cum = nn(tri, log, HIGHEST)
        cum_t = cum.T
        u = x * spread(step, SBLK)
        u_low = u.astype(BF16)
        inner = nt(c_low, b_low)
        state = state_out[pl.ds(0, XW), :]
        entry_out[k] = state
        parts = []
        for h in range(XW // HP):
            decay = jnp.exp(
                jnp.where(lower, cum[:, h : h + 1] - cum_t[h : h + 1, :], MASKED)
            )
            parts.append(nn((inner * decay).astype(BF16), u_low[:, h * HP : (h + 1) * HP]))
        carried = nt(c_low, state.astype(BF16)) * spread(jnp.exp(cum), SBLK)
        y_out[pl.ds(base, SBLK), :] = (
            jnp.concatenate(parts, axis=1) + carried + spread(par[2:3, :], 1) * x
        )
        last = cum[SBLK - 1 : SBLK, :]
        tail = (u * spread(jnp.exp(last - cum), SBLK)).astype(BF16)
        shrink = jnp.concatenate(
            [
                jnp.broadcast_to(jnp.exp(last[:, h : h + 1]), (HP, NS))
                for h in range(XW // HP)
            ],
            axis=0,
        )
        state_out[pl.ds(0, XW), :] = state * shrink + tn(tail, b_low)
        c_out[pl.ds(base, SBLK), :] = c_low
        cum_out[pl.ds(base, SBLK), :] = cum + before
        before = before + last
    state_out[pl.ds(XW, 8), :] = jnp.broadcast_to(before, (8, 128))


def ssd_forward_call(slab, halo, taps, par):
    length = slab.shape[0]
    return pl.pallas_call(
        ssd_forward,
        out_shape=(
            jax.ShapeDtypeStruct((length, XW), F32),
            jax.ShapeDtypeStruct((XW + 8, NS), F32),
            jax.ShapeDtypeStruct((length, NS), BF16),
            jax.ShapeDtypeStruct((length, 128), F32),
            jax.ShapeDtypeStruct((length // SBLK, XW, NS), F32),
        ),
        scratch_shapes=[pltpu.VMEM((length + HALO, CW), F32)],
        compiler_params=pltpu.CompilerParams(vmem_limit_bytes=VMEM_LIMIT),
        cost_estimate=pl.CostEstimate(
            flops=8_000_000_000, bytes_accessed=8_000_000, transcendentals=1_000_000
        ),
        name="ssd_forward",
    )(slab, halo, taps, par)


def shrink_rows(log_row):
    return jnp.concatenate(
        [jnp.broadcast_to(jnp.exp(log_row[:, h : h + 1]), (HP, NS)) for h in range(XW // HP)],
        axis=0,
    )


def ssd_join(y, c, cum, near, mid, far, attended, out, entering):
    state = near[pl.ds(0, XW), :] + shrink_rows(near[XW : XW + 1, :]) * (
        mid[pl.ds(0, XW), :] + shrink_rows(mid[XW : XW + 1, :]) * far[pl.ds(0, XW), :]
    )
    entering[...] = state
    state_low = state.astype(BF16)
    rows = y.shape[0]
    for base in range(0, rows, SBLK):
        at = pl.ds(base, SBLK)
        mixed = y[at, :] + nt(c[at, :], state_low) * spread(jnp.exp(cum[at, :]), SBLK)
        out[at, :] = jnp.concatenate([mixed, attended[at, :]], axis=1).astype(BF16)


def ssd_join_call(y, c, cum, near, mid, far, attended):
    return pl.pallas_call(
        ssd_join,
        out_shape=(
            jax.ShapeDtypeStruct((y.shape[0], XW + HP), BF16),
            jax.ShapeDtypeStruct((XW, NS), F32),
        ),
        compiler_params=pltpu.CompilerParams(vmem_limit_bytes=VMEM_LIMIT),
        name="ssd_join",
    )(y, c, cum, near, mid, far, attended)


def ssd_entry_gradient(grad, c, cum, out):
    rows = grad.shape[0]
    total = jnp.zeros((XW, NS), F32)
    for base in range(0, rows, SBLK):
        at = pl.ds(base, SBLK)
        scaled = grad[at, :XW].astype(F32) * spread(jnp.exp(cum[at, :]), SBLK)
        total = total + tn(scaled.astype(BF16), c[at, :])
    out[pl.ds(0, XW), :] = total
    out[pl.ds(XW, 8), :] = jnp.broadcast_to(cum[rows - 1 : rows, :], (8, 128))


def ssd_entry_gradient_call(grad, c, cum):
    return pl.pallas_call(
        ssd_entry_gradient,
        out_shape=jax.ShapeDtypeStruct((XW + 8, NS), F32),
        compiler_params=pltpu.CompilerParams(vmem_limit_bytes=VMEM_LIMIT),
        name="ssd_entry_gradient",
    )(grad, c, cum)


def ssd_backward(
    slab, halo, taps, par, grad, entry, cum_all, entering, near, mid, far,
    grad_in, grad_dt, grad_rim, grad_taps, grad_par, ext, gpre,
):
    length = slab.shape[0]
    chunks = length // SBLK
    ext[pl.ds(0, HALO), :] = halo[...].astype(F32)
    ext[pl.ds(HALO, length), :] = slab[:, :CW].astype(F32)
    gpre[pl.ds(length, HALO), :] = jnp.zeros((HALO, CW), F32)
    weights = taps[...]
    lower = iota((SBLK, SBLK), 0) >= iota((SBLK, SBLK), 1)
    tri = lower.astype(F32)
    upper = (iota((SBLK, SBLK), 0) <= iota((SBLK, SBLK), 1)).astype(F32)
    hsum = head_sum_matrix()
    rate = jnp.exp(par[0:1, :])
    skip = spread(par[2:3, :], 1)
    enter = entering[...]
    later = near[pl.ds(0, XW), :] + shrink_rows(near[XW : XW + 1, :]) * (
        mid[pl.ds(0, XW), :] + shrink_rows(mid[XW : XW + 1, :]) * far[pl.ds(0, XW), :]
    )
    g_decay = jnp.zeros((1, 128), F32)
    g_bias = jnp.zeros((1, 128), F32)
    g_skip = jnp.zeros((1, 128), F32)
    for k in reversed(range(chunks)):
        base = k * SBLK
        at = pl.ds(base, SBLK)
        pre = conv_pre(ext, weights, base)
        sig = jax.nn.sigmoid(pre)
        conv = pre * sig
        b_low = conv[:, :NS].astype(BF16)
        c_low = conv[:, NS : 2 * NS].astype(BF16)
        x = conv[:, 2 * NS :]
        raw, step, log = step_and_log(slab, par, base)
        cum = nn(tri, log, HIGHEST)
        cum_t = cum.T
        last = cum[SBLK - 1 : SBLK, :]
        step_wide = spread(step, SBLK)
        u_low = (x * step_wide).astype(BF16)
        u = u_low.astype(F32)
        gy_low = grad[at, :XW]
        gy = gy_low.astype(F32)
        if k:
            state = entry[k] + shrink_rows(cum_all[base - 1 : base, :]) * enter
        else:
            state = enter
        state_low = state.astype(BF16)
        later_low = later.astype(BF16)
        inner = nt(c_low, b_low)
        g_inner = jnp.zeros((SBLK, SBLK), F32)
        y_parts, gu_parts = [], []
        for h in range(XW // HP):
            lanes = slice(h * HP, (h + 1) * HP)
            decay = jnp.exp(
                jnp.where(lower, cum[:, h : h + 1] - cum_t[h : h + 1, :], MASKED)
            )
            kernel = (inner * decay).astype(BF16)
            y_parts.append(nn(kernel, u_low[:, lanes]))
            gu_parts.append(tn(kernel, gy_low[:, lanes]))
            g_inner = g_inner + nt(gy_low[:, lanes], u_low[:, lanes]) * decay
        g_inner_low = g_inner.astype(BF16)
        enter_wide = spread(jnp.exp(cum), SBLK)
        tail_wide = spread(jnp.exp(last - cum), SBLK)
        gy_scaled = (gy * enter_wide).astype(BF16)
        u_scaled = (u * tail_wide).astype(BF16)
        y = jnp.concatenate(y_parts, axis=1) + nt(c_low, state_low) * enter_wide
        tail = nt(b_low, later_low) * tail_wide
        gu = jnp.concatenate(gu_parts, axis=1) + tail
        gc = nn(g_inner_low, b_low) + nn(gy_scaled, state_low)
        gb = tn(g_inner_low, c_low) + nn(u_scaled, later_low)
        shrink = shrink_rows(last)
        both = nn(gy * y - u * gu, hsum, HIGHEST)
        tail_sum = jnp.sum(nn(u * tail, hsum, HIGHEST), axis=0, keepdims=True)
        across = jnp.sum(
            jnp.sum(later * state * shrink, axis=1, keepdims=True) * hsum, axis=0, keepdims=True
        )
        g_log = nn(upper, both, HIGHEST) + tail_sum + across
        g_step = nn(x * gu, hsum, HIGHEST) - rate * g_log
        g_raw = g_step * jax.nn.sigmoid(raw)
        g_decay = g_decay + jnp.sum(g_log * log, axis=0, keepdims=True)
        g_bias = g_bias + jnp.sum(g_raw, axis=0, keepdims=True)
        g_skip = g_skip + jnp.sum(nn(gy * x, hsum, HIGHEST), axis=0, keepdims=True)
        grad_dt[at, :] = g_raw
        g_conv = jnp.concatenate([gb, gc, step_wide * gu + skip * gy], axis=1)
        gpre[at, :] = g_conv * (sig + conv * (1.0 - sig))
        later = shrink * later + tn(gy_scaled, c_low)
    for k in range(chunks):
        base = k * SBLK
        acc = gpre[pl.ds(base + 3, SBLK), :] * weights[0:1, :]
        for tap in range(1, KW):
            acc = acc + gpre[pl.ds(base + 3 - tap, SBLK), :] * weights[tap : tap + 1, :]
        grad_in[pl.ds(base, SBLK), :] = acc
    first = gpre[pl.ds(0, 8), :]
    rim = jnp.zeros((8, CW), F32)
    rows = iota((8, CW), 0)
    for back in range(1, KW):
        term = jnp.zeros((1, CW), F32)
        for tap in range(KW):
            t = 3 - tap - back
            if 0 <= t:
                term = term + first[t : t + 1, :] * weights[tap : tap + 1, :]
        rim = jnp.where(rows == 8 - back, term, rim)
    grad_rim[...] = rim
    g_taps = jnp.zeros((8, CW), F32)
    rows = iota((8, CW), 0)
    for tap in range(KW):
        total = jnp.zeros((1, CW), F32)
        for k in range(chunks):
            base = k * SBLK
            total = total + jnp.sum(
                gpre[pl.ds(base, SBLK), :] * ext[pl.ds(base + HALO - 3 + tap, SBLK), :],
                axis=0,
                keepdims=True,
            )
        g_taps = jnp.where(rows == tap, total, g_taps)
    grad_taps[...] = g_taps
    rows = iota((8, 128), 0)
    grad_par[...] = jnp.where(
        rows == 0, g_decay, jnp.where(rows == 1, g_bias, jnp.where(rows == 2, g_skip, 0.0))
    )


def ssd_backward_call(slab, halo, taps, par, grad, entry, cum, entering, near, mid, far):
    length = slab.shape[0]
    return pl.pallas_call(
        ssd_backward,
        out_shape=(
            jax.ShapeDtypeStruct((length, CW), F32),
            jax.ShapeDtypeStruct((length, 128), F32),
            jax.ShapeDtypeStruct((8, CW), F32),
            jax.ShapeDtypeStruct((8, CW), F32),
            jax.ShapeDtypeStruct((8, 128), F32),
        ),
        scratch_shapes=[
            pltpu.VMEM((length + HALO, CW), F32),
            pltpu.VMEM((length + HALO, CW), F32),
        ],
        compiler_params=pltpu.CompilerParams(vmem_limit_bytes=VMEM_LIMIT),
        cost_estimate=pl.CostEstimate(
            flops=20_000_000_000, bytes_accessed=12_000_000, transcendentals=2_000_000
        ),
        name="ssd_backward",
    )(slab, halo, taps, par, grad, entry, cum, entering, near, mid, far)


QB = 256
KB = 512


def place_keys(rank, parts, kv):
    length = parts[0].shape[0]
    for back, part in enumerate(parts):

        @pl.when(rank >= back)
        def _():
            kv[pl.ds(pl.multiple_of((rank - back) * length, length), length), :] = part[...]


def attend_forward(rank_ref, slab, near, mid, far, out, lse, kv, own):
    length = slab.shape[0]
    rank = rank_ref[0]
    offset = rank * length
    scale = HP**-0.5
    ahead = iota((QB, KB), 0) - iota((QB, KB), 1)
    own[...] = slab[:, KV_AT:DT_AT]
    place_keys(rank, (own, near, mid, far), kv)

    def q_step(i, _):
        at = pl.ds(pl.multiple_of(i * QB, QB), QB)
        q_blk = (slab[at, Q_AT:KV_AT].astype(F32) * scale).astype(BF16)
        first = offset + i * QB

        def block(j, carry, masked):
            top, total, acc = carry
            at = pl.ds(pl.multiple_of(j * KB, KB), KB)
            s = nt(q_blk, kv[at, :HP])
            if masked:
                s = jnp.where(ahead >= j * KB - first, s, MASKED)
            new = jnp.maximum(top, jnp.max(s, axis=1, keepdims=True))
            p = jnp.exp(s - new)
            fade = jnp.exp(top - new)
            total = total * fade + jnp.sum(p, axis=1, keepdims=True)
            acc = acc * fade + nn(p.astype(BF16), kv[at, HP:])
            return new, total, acc

        whole = first // KB
        carry = (
            jnp.full((QB, 1), MASKED, F32),
            jnp.zeros((QB, 1), F32),
            jnp.zeros((QB, HP), F32),
        )
        carry = lax.fori_loop(0, whole, lambda j, c: block(j, c, False), carry)
        top, total, acc = block(whole, carry, True)
        out[at, :] = acc / total
        lse[at, :] = jnp.broadcast_to(top + jnp.log(total), (QB, 128))
        return 0

    lax.fori_loop(0, length // QB, q_step, 0)


def attend_forward_call(rank, slab, near, mid, far):
    length = slab.shape[0]
    vm = pl.BlockSpec(memory_space=pltpu.VMEM)
    return pl.pallas_call(
        attend_forward,
        in_specs=[pl.BlockSpec(memory_space=pltpu.SMEM)] + [vm] * 4,
        out_shape=(
            jax.ShapeDtypeStruct((length, HP), F32),
            jax.ShapeDtypeStruct((length, 128), F32),
        ),
        scratch_shapes=[
            pltpu.VMEM((4 * length, 2 * HP), BF16),
            pltpu.VMEM((length, 2 * HP), BF16),
        ],
        compiler_params=pltpu.CompilerParams(vmem_limit_bytes=VMEM_LIMIT),
        cost_estimate=pl.CostEstimate(
            flops=8_000_000_000, bytes_accessed=4_000_000, transcendentals=4_000_000
        ),
        name="attend_forward",
    )(rank, slab, near, mid, far)


def attend_backward(
    rank_ref, slab, near, mid, far, g, out, lse, gq, g_own, g_near, g_mid, g_far, kv, own, acc
):
    length = slab.shape[0]
    rank = rank_ref[0]
    offset = rank * length
    scale = HP**-0.5
    ahead = iota((QB, KB), 0) - iota((QB, KB), 1)
    own[...] = slab[:, KV_AT:DT_AT]
    place_keys(rank, (own, near, mid, far), kv)
    acc[...] = jnp.zeros_like(acc)

    def q_step(i, _):
        at_q = pl.ds(pl.multiple_of(i * QB, QB), QB)
        q_blk = (slab[at_q, Q_AT:KV_AT].astype(F32) * scale).astype(BF16)
        g_low = g[at_q, XW:]
        delta = jnp.sum(g_low.astype(F32) * out[at_q, :], axis=1, keepdims=True)
        log_total = lse[at_q, 0:1]
        first = offset + i * QB

        def block(j, gq_acc, masked):
            at = pl.ds(pl.multiple_of(j * KB, KB), KB)
            k_blk = kv[at, :HP]
            s = nt(q_blk, k_blk)
            if masked:
                s = jnp.where(ahead >= j * KB - first, s, MASKED)
            p = jnp.exp(s - log_total)
            dp = nt(g_low, kv[at, HP:])
            ds = (p * (dp - delta)).astype(BF16)
            acc[at, :] += jnp.concatenate([tn(ds, q_blk), tn(p.astype(BF16), g_low)], axis=1)
            return gq_acc + nn(ds, k_blk)

        whole = first // KB
        carry = jnp.zeros((QB, HP), F32)
        carry = lax.fori_loop(0, whole, lambda j, c: block(j, c, False), carry)
        gq[at_q, :] = block(whole, carry, True) * scale
        return 0

    lax.fori_loop(0, length // QB, q_step, 0)
    for back, target in enumerate((g_own, g_near, g_mid, g_far)):

        @pl.when(rank >= back)
        def _():
            at = pl.ds(pl.multiple_of((rank - back) * length, length), length)
            target[...] = acc[at, :].astype(target.dtype)

        @pl.when(rank < back)
        def _():
            target[...] = jnp.zeros_like(target)


def attend_backward_call(rank, slab, near, mid, far, g, out, lse):
    length = slab.shape[0]
    vm = pl.BlockSpec(memory_space=pltpu.VMEM)
    keys = jax.ShapeDtypeStruct((length, 2 * HP), BF16)
    return pl.pallas_call(
        attend_backward,
        in_specs=[pl.BlockSpec(memory_space=pltpu.SMEM)] + [vm] * 7,
        out_shape=(
            jax.ShapeDtypeStruct((length, HP), F32),
            jax.ShapeDtypeStruct((length, 2 * HP), F32),
            keys,
            keys,
            keys,
        ),
        scratch_shapes=[
            pltpu.VMEM((4 * length, 2 * HP), BF16),
            pltpu.VMEM((length, 2 * HP), BF16),
            pltpu.VMEM((4 * length, 2 * HP), F32),
        ],
        compiler_params=pltpu.CompilerParams(vmem_limit_bytes=VMEM_LIMIT),
        cost_estimate=pl.CostEstimate(
            flops=20_000_000_000, bytes_accessed=4_000_000, transcendentals=4_000_000
        ),
        name="attend_backward",
    )(rank, slab, near, mid, far, g, out, lse)


CORE_ROWS = 16
PARTS = (0, 768, 1536, 2176)
ORDERS = ((0, 1, 2), (1, 2, 0), (2, 0, 1))
TORUS = ("fs", "cp", "ux")


def sum_over_devices(
    left, right, small, out, small_out,
    left_in, right_in, part0, part1, part2, got10, got11, got12, mid0, mid1, mid2,
    got20, got21, got22, end0, end1, end2, got30, got31, got32, done, done_in, small_in, small_core,
    core_send, core_recv, send, recv, small_send, small_recv,
):
    mesh_kind = pl.DeviceIdType.MESH
    core = lax.axis_index("uc")
    place = [lax.axis_index(a) for a in TORUS]
    other = {"uc": 1 - core}
    half = right.shape[1] // 2
    rows = left.shape[0]

    def peer(axis, shift):
        return {TORUS[axis]: lax.rem(place[axis] + shift, 4)}

    barrier = pltpu.get_barrier_semaphore()
    pl.semaphore_signal(barrier, inc=1, device_id=other, device_id_type=mesh_kind)
    for axis in range(3):
        for shift in (1, 2, 3):
            pl.semaphore_signal(
                barrier, inc=1, device_id=peer(axis, shift), device_id_type=mesh_kind
            )
    pl.semaphore_wait(barrier, 10)

    def remote(src, dst, send_sem, recv_sem, target):
        copy = pltpu.make_async_remote_copy(
            src_ref=src, dst_ref=dst, send_sem=send_sem, recv_sem=recv_sem,
            device_id=target, device_id_type=mesh_kind,
        )
        copy.start()
        return copy

    theirs = pl.ds(pl.multiple_of((1 - core) * half, 128), half)
    ours = pl.ds(pl.multiple_of(core * half, 128), half)
    core_copies = [
        remote(left, left_in, core_send.at[0], core_recv.at[0], other),
        remote(right.at[:, theirs], right_in, core_send.at[1], core_recv.at[1], other),
        remote(small, small_core, core_send.at[2], core_recv.at[2], other),
    ]
    for copy in core_copies:
        copy.wait()

    parts = (part0, part1, part2)
    got1, got2, got3 = (got10, got11, got12), (got20, got21, got22), (got30, got31, got32)
    mids, ends = (mid0, mid1, mid2), (end0, end1, end2)
    lefts = [(left[:, f * 256 : (f + 1) * 256], left_in[:, f * 256 : (f + 1) * 256]) for f in range(4)]
    first = []
    for p in range(3):
        width = PARTS[p + 1] - PARTS[p]
        at = pl.ds(pl.multiple_of(core * half + PARTS[p], 128), width)
        mine, their = right[:, at], right_in[:, PARTS[p] : PARTS[p + 1]]
        rights = jnp.concatenate([mine, their], axis=0)
        for f in range(4):
            block = tn(jnp.concatenate(lefts[f], axis=0), rights).astype(BF16)
            for c in range(4):
                for x in range(4):
                    where = (f, c, x)
                    a0, a1, a2 = (where[a] for a in ORDERS[p])
                    start = (c * 4 + x) * CORE_ROWS
                    parts[p][a0, a1, a2] = block[start : start + CORE_ROWS]
        axis = ORDERS[p][0]
        first.append(
            [
                remote(
                    parts[p].at[lax.rem(place[axis] + shift, 4)], got1[p].at[shift - 1],
                    send.at[p, 0, shift - 1], recv.at[p, 0, shift - 1], peer(axis, shift),
                )
                for shift in (1, 2, 3)
            ]
        )

    total = small[...] + small_core[...]
    for axis in range(3):
        small_in[axis, place[axis]] = total
        copies = [
            remote(
                small_in.at[axis, place[axis]], small_in.at[axis, place[axis]],
                small_send.at[axis, shift - 1], small_recv.at[axis, shift - 1], peer(axis, shift),
            )
            for shift in (1, 2, 3)
        ]
        for copy in copies:
            copy.wait()
        total = (small_in[axis, 0] + small_in[axis, 1]) + (small_in[axis, 2] + small_in[axis, 3])
    small_out[...] = total

    def add(source, slots, index):
        acc = source[index].astype(F32)
        for s in range(3):
            acc = acc + slots[s].astype(F32)
        return acc

    second = []
    for p in range(3):
        for copy in first[p]:
            copy.wait()
        for i in range(4):
            acc = parts[p][place[ORDERS[p][0]], i].astype(F32)
            for s in range(3):
                acc = acc + got1[p][s, i].astype(F32)
            mids[p][i] = acc.astype(BF16)
        axis = ORDERS[p][1]
        second.append(
            [
                remote(
                    mids[p].at[lax.rem(place[axis] + shift, 4)], got2[p].at[shift - 1],
                    send.at[p, 1, shift - 1], recv.at[p, 1, shift - 1], peer(axis, shift),
                )
                for shift in (1, 2, 3)
            ]
        )
    third = []
    for p in range(3):
        for copy in second[p]:
            copy.wait()
        ends[p][...] = add(mids[p], got2[p], place[ORDERS[p][1]]).astype(BF16)
        axis = ORDERS[p][2]
        third.append(
            [
                remote(
                    ends[p].at[lax.rem(place[axis] + shift, 4)], got3[p].at[shift - 1],
                    send.at[p, 2, shift - 1], recv.at[p, 2, shift - 1], peer(axis, shift),
                )
                for shift in (1, 2, 3)
            ]
        )
    for p in range(3):
        for copy in third[p]:
            copy.wait()
        done[:, PARTS[p] : PARTS[p + 1]] = add(ends[p], got3[p], place[ORDERS[p][2]])
    keep = pl.ds(pl.multiple_of(core * 8, 8), 8)
    give = pl.ds(pl.multiple_of((1 - core) * 8, 8), 8)
    last = remote(done.at[give, :], done_in, core_send.at[3], core_recv.at[3], other)
    out[:, ours] = done[keep, :]
    last.wait()
    out[:, theirs] = done_in[...]


def sum_over_devices_call(left, right, small):
    half = right.shape[1] // 2
    widths = [PARTS[p + 1] - PARTS[p] for p in range(3)]

    def blocks(*lead):
        return [pltpu.VMEM(lead + (CORE_ROWS, w), BF16) for w in widths]

    return pl.pallas_call(
        sum_over_devices,
        in_specs=[pl.BlockSpec(memory_space=pltpu.VMEM)] * 3,
        out_specs=[pl.BlockSpec(memory_space=pltpu.VMEM)] * 2,
        out_shape=(
            jax.ShapeDtypeStruct((8, 2 * half), F32),
            jax.ShapeDtypeStruct(small.shape, F32),
        ),
        scratch_shapes=[
            pltpu.VMEM(left.shape, BF16),
            pltpu.VMEM((left.shape[0], half), BF16),
            *blocks(4, 4, 4),
            *blocks(3, 4, 4),
            *blocks(4, 4),
            *blocks(3, 4),
            *blocks(4),
            *blocks(3),
            pltpu.VMEM((CORE_ROWS, half), F32),
            pltpu.VMEM((8, half), F32),
            pltpu.VMEM((3, 4) + small.shape, F32),
            pltpu.VMEM(small.shape, F32),
            pltpu.SemaphoreType.DMA((4,)),
            pltpu.SemaphoreType.DMA((4,)),
            pltpu.SemaphoreType.DMA((3, 3, 3)),
            pltpu.SemaphoreType.DMA((3, 3, 3)),
            pltpu.SemaphoreType.DMA((3, 3)),
            pltpu.SemaphoreType.DMA((3, 3)),
        ],
        compiler_params=pltpu.CompilerParams(
            vmem_limit_bytes=VMEM_LIMIT, collective_id=0, has_side_effects=True
        ),
        cost_estimate=pl.CostEstimate(
            flops=1_200_000_000, bytes_accessed=4_000_000, transcendentals=0
        ),
        name="sum_over_devices",
    )(left, right, small)


HM = 24
GROUPS = 8
HEADS = 8
KEY_HEADS = 2
FF = 2048
DS = 1536
PROJ = 4120
PROJ_WIDE = 4352
EPSILON = 1e-05
TOKEN_AXES = ("fs", "cp", "ux", "uc")


def rms_norm(values, norm_gain):
    return (
        values * lax.rsqrt(jnp.mean(values * values, axis=-1, keepdims=True) + EPSILON) * norm_gain
    )


def gated_norm(mixed_heads, gate_pre, norm_gain):
    return rms_norm(mixed_heads * jax.nn.silu(gate_pre), norm_gain)


def from_behind(block, distance):
    return lax.ppermute(block, "cp", [(i - distance, i) for i in range(distance, 4)])


def from_ahead(block, distance):
    return lax.ppermute(block, "cp", [(i, i - distance) for i in range(distance, 4)])


def other_core(block):
    return lax.ppermute(block, "uc", [(0, 1), (1, 0)])


def columns_half(block, half):
    width = block.shape[1] // 2
    return lax.dynamic_slice_in_dim(block, half * width, width, 1)


def gather_rows(shard, core):
    rows = shard.shape[0] // 2
    mine = lax.dynamic_slice_in_dim(shard, core * rows, rows, 0)
    place = lax.axis_index("fs")
    got = jnp.stack(
        [mine]
        + [lax.ppermute(mine, "fs", [(i, (i + s) % 4) for i in range(4)]) for s in (1, 2, 3)]
    )
    order = jnp.mod(place - jnp.arange(4), 4)
    ours = jnp.take(got, order, axis=0)
    return ours, other_core(ours)


def gather_all(shard, at):
    rows = shard.shape[0] // 32
    return lax.all_gather(
        lax.dynamic_slice_in_dim(shard, at * rows, rows, 0), TOKEN_AXES, axis=0, tiled=True
    )


def both_cores(left, right, core):
    lefts = jnp.concatenate([left, other_core(left)], axis=0)
    rights = jnp.concatenate(
        [columns_half(right, core), other_core(columns_half(right, 1 - core))], axis=0
    )
    return lefts, rights


def core_halves(rows, core):
    r = rows.shape[0] // 2
    mine = lax.dynamic_slice_in_dim(rows, core * r, r, 0)
    theirs = other_core(lax.dynamic_slice_in_dim(rows, (1 - core) * r, r, 0))
    return jnp.concatenate(
        [jnp.where(core == 0, mine, theirs), jnp.where(core == 0, theirs, mine)], axis=1
    ).astype(F32)


def weight_gradients(pairs, core):
    blocks = []
    for left, right in pairs:
        lefts, rights = both_cores(left, right, core)
        for at in range(0, rights.shape[1], 512):
            part = tn(lefts, rights[:, at : at + 512]).astype(BF16)
            blocks.append(part.reshape(64, part.shape[0] // 64, 512))
    total = jnp.concatenate(blocks, axis=1)
    for axis in ("fs", "cp", "ux"):
        total = lax.psum_scatter(total, axis, scatter_dimension=0, tiled=True)
    total = total[0]
    results, at = [], 0
    for left, right in pairs:
        r = left.shape[1] // 64
        count = right.shape[1] // 1024
        whole = jnp.concatenate(
            [total[at + i * r : at + (i + 1) * r] for i in range(count)], axis=1
        )
        at += count * r
        results.append(core_halves(whole, core))
    return results


def shards(
    tokens,
    norm_in,
    norm_mid,
    mamba_gain,
    conv_weight,
    decay_log,
    dt_bias,
    skip_gain,
    w_in,
    w_mout,
    w_aout,
    w_gu,
    w_down,
    grad_out,
):
    part_rank = lax.axis_index("cp")
    core = lax.axis_index("uc")
    group = lax.axis_index("ux") * 2 + core
    rows = tokens.shape[0]
    length = GROUPS * rows
    heads = HM // GROUPS
    at = part_rank * GROUPS + group
    in_ours, in_theirs = gather_rows(w_in, core)
    gu_ours, gu_theirs = gather_rows(w_gu, core)
    full_mout, full_aout, full_down = (gather_all(w, at) for w in (w_mout, w_aout, w_down))

    def halves(block):
        pieces = block.reshape(rows, 4, 2, block.shape[1] // 8)
        picked = [
            lax.dynamic_index_in_dim(pieces, which, 2, False).reshape(rows, block.shape[1] // 2)
            for which in (core, 1 - core)
        ]
        return picked

    def times_halves(block, ours, theirs):
        own, rest = halves(block)
        width = ours.shape[-1]
        return nn(own, ours.reshape(-1, width)) + nn(rest, theirs.reshape(-1, width))

    def times_halves_transposed(block, ours, theirs):
        width = ours.shape[-1]
        own = nt(block, ours.reshape(-1, width)).reshape(rows, 4, -1)
        rest = nt(block, theirs.reshape(-1, width)).reshape(rows, 4, -1)
        pieces = jnp.where(core == 0, jnp.stack([own, rest], 2), jnp.stack([rest, own], 2))
        return pieces.reshape(rows, -1)

    def to_groups(blocks):
        return lax.all_to_all(blocks, ("ux", "uc"), split_axis=0, concat_axis=0, tiled=True)

    resid_in = tokens.astype(F32)
    normed_f, in_back = jax.vjp(rms_norm, resid_in, norm_in)
    normed_in = normed_f.astype(BF16)
    projected = times_halves(normed_in, in_ours, in_theirs)
    gate_pre = projected[:, :DS]
    low = projected[:, DS:].astype(BF16)
    q_at = DS + 2 * NS + HM
    k_at = q_at + HEADS * HP
    v_at = k_at + KEY_HEADS * HP
    blocks = []
    for g in range(GROUPS):
        key = g * KEY_HEADS // GROUPS
        blocks.append(
            jnp.concatenate(
                [
                    low[:, DS : DS + 2 * NS],
                    low[:, g * XW : (g + 1) * XW],
                    low[:, q_at + g * HP : q_at + (g + 1) * HP],
                    low[:, k_at + key * HP : k_at + (key + 1) * HP],
                    low[:, v_at + key * HP : v_at + (key + 1) * HP],
                    low[:, DS + 2 * NS + g * heads : DS + 2 * NS + (g + 1) * heads],
                    jnp.zeros((rows, 128 - heads), BF16),
                ],
                axis=1,
            )
        )
    slab = to_groups(jnp.stack(blocks)).reshape(length, DT_AT + 128)

    taps = jnp.concatenate(
        [conv_weight[:, DS:], lax.dynamic_slice_in_dim(conv_weight, group * XW, XW, 1)], axis=1
    )
    taps = jnp.pad(taps, ((0, 8 - KW), (0, 0)))
    per_head = jnp.stack([decay_log, dt_bias, skip_gain])
    par = jnp.pad(
        lax.dynamic_slice_in_dim(per_head, group * heads, heads, 1), ((0, 5), (0, 128 - heads))
    )
    rank = part_rank.astype(jnp.int32).reshape(1)

    halo = from_behind(slab[length - HALO :, :CW], 1)
    own_keys = slab[:, KV_AT:DT_AT]
    keys = [from_behind(own_keys, d) for d in (1, 2, 3)]
    y, state, c_low, cum, entry = ssd_forward_call(slab, halo, taps, par)
    states = [from_behind(state, d) for d in (1, 2, 3)]
    attended, lse = attend_forward_call(rank, slab, *keys)
    joined, entering = ssd_join_call(y, c_low, cum, *states, attended)
    tok = to_groups(joined.reshape(GROUPS, rows, XW + HP)).transpose(1, 0, 2)
    mixed_tok = tok[:, :, :XW].reshape(rows, DS)
    attended_tok = tok[:, :, XW:].reshape(rows, HEADS * HP)

    branch_f, gate_back = jax.vjp(gated_norm, mixed_tok.astype(F32), gate_pre, mamba_gain)
    branch_low = branch_f.astype(BF16)
    resid_mid = resid_in + nn(branch_low, full_mout) + nn(attended_tok, full_aout)
    normed_mid_f, mid_back = jax.vjp(rms_norm, resid_mid, norm_mid)
    normed_mid = normed_mid_f.astype(BF16)
    gate_up = times_halves(normed_mid, gu_ours, gu_theirs)
    gate_half = gate_up[:, :FF]
    up_half = gate_up[:, FF:]
    sigmoid_gate = jax.nn.sigmoid(gate_half)
    hidden = (gate_half * sigmoid_gate * up_half).astype(BF16)
    layer_out = (resid_mid + nn(hidden, full_down)).astype(BF16)
    grad_hidden = nt(grad_out, full_down)
    grad_gate = grad_hidden * up_half * sigmoid_gate * (1.0 + gate_half * (1.0 - sigmoid_gate))
    grad_up = grad_hidden * gate_half * sigmoid_gate
    grad_gate_up = jnp.concatenate([grad_gate, grad_up], axis=1).astype(BF16)
    resid_back, grad_norm_mid = mid_back(
        times_halves_transposed(grad_gate_up, gu_ours, gu_theirs)
    )
    grad_resid = grad_out.astype(F32) + resid_back
    resid_low = grad_resid.astype(BF16)
    grad_mixed, grad_gate_pre, grad_mamba_gain = gate_back(nt(resid_low, full_mout))
    grad_attended = nt(resid_low, full_aout)
    grad_blocks = jnp.concatenate(
        [
            grad_mixed.astype(BF16).reshape(rows, GROUPS, XW),
            grad_attended.astype(BF16).reshape(rows, GROUPS, HP),
        ],
        axis=2,
    ).transpose(1, 0, 2)
    grad = to_groups(grad_blocks).reshape(length, XW + HP)
    grad_gu, grad_down, grad_mout, grad_aout = weight_gradients(
        [
            (normed_mid, grad_gate_up),
            (hidden, grad_out),
            (branch_low, resid_low),
            (attended_tok, resid_low),
        ],
        core,
    )

    entry_gradient = ssd_entry_gradient_call(grad, c_low, cum)
    later = [from_ahead(entry_gradient, d) for d in (1, 2, 3)]
    grad_query, key_own, *key_parts = attend_backward_call(rank, slab, *keys, grad, attended, lse)
    key_parts = [from_ahead(p, d + 1) for d, p in enumerate(key_parts)]
    grad_in_cols, grad_dt, rim, grad_taps, grad_par = ssd_backward_call(
        slab, halo, taps, par, grad, entry, cum, entering, *later
    )
    rim = from_ahead(rim, 1)
    grad_cols = jnp.concatenate(
        [grad_in_cols[: length - 8], grad_in_cols[length - 8 :] + rim], axis=0
    )
    grad_keys = key_own + sum(p.astype(F32) for p in key_parts)
    back = jnp.concatenate(
        [grad_cols.astype(BF16), grad_query.astype(BF16), grad_keys.astype(BF16), grad_dt.astype(BF16)],
        axis=1,
    )
    back = to_groups(back.reshape(GROUPS, rows, DT_AT + 128))
    grad_x = back[:, :, 2 * NS : CW].transpose(1, 0, 2).reshape(rows, DS)
    grad_bc = jnp.sum(back[:, :, : 2 * NS].astype(F32), axis=0).astype(BF16)
    grad_q = back[:, :, Q_AT:KV_AT].transpose(1, 0, 2).reshape(rows, HEADS * HP)
    shared = back[:, :, KV_AT:DT_AT].astype(F32).reshape(KEY_HEADS, GROUPS // KEY_HEADS, rows, 2, HP)
    grad_kv = jnp.sum(shared, axis=1).transpose(1, 2, 0, 3).reshape(rows, 2 * KEY_HEADS * HP)
    grad_dt_tok = back[:, :, DT_AT : DT_AT + heads].transpose(1, 0, 2).reshape(rows, HM)
    grad_proj = jnp.concatenate(
        [
            grad_gate_pre.astype(BF16),
            grad_x,
            grad_bc,
            grad_dt_tok,
            grad_q,
            grad_kv.astype(BF16),
            jnp.zeros((rows, PROJ_WIDE - PROJ), BF16),
        ],
        axis=1,
    )
    tokens_back, grad_norm_in = in_back(
        times_halves_transposed(grad_proj[:, :PROJ], in_ours, in_theirs)
    )
    grad_tokens = grad_resid + tokens_back

    conv_full = jnp.concatenate(
        [
            lax.dynamic_update_slice_in_dim(
                jnp.zeros((KW, DS), F32), grad_taps[:KW, 2 * NS :], group * XW, 1
            ),
            grad_taps[:KW, : 2 * NS],
        ],
        axis=1,
    )
    head_full = lax.dynamic_update_slice_in_dim(
        jnp.zeros((3, HM), F32), grad_par[:3, :heads], group * heads, 1
    )
    parts = [
        a.reshape(-1) for a in (grad_norm_in, grad_norm_mid, grad_mamba_gain, conv_full, head_full)
    ]
    flat = jnp.concatenate(parts)
    flat = jnp.pad(flat, (0, 16 * 1024 - flat.shape[0])).reshape(16, 1024)
    grad_in, flat = sum_over_devices_call(normed_in, grad_proj, flat)
    flat = flat.reshape(-1)
    small, at = [], 0
    for shape in ((1024,), (1024,), (DS,), (KW, DS + 2 * NS), (3, HM)):
        size = math.prod(shape)
        small.append(flat[at : at + size].reshape(shape))
        at += size
    return (
        layer_out,
        grad_tokens,
        small[0],
        small[1],
        small[2],
        small[3],
        small[4][0],
        small[4][1],
        small[4][2],
        grad_in[:, :PROJ],
        grad_mout,
        grad_aout,
        grad_gu,
        grad_down,
    )


def solution(mesh):
    fine = Mesh(mesh.devices.reshape(4, 4, 4, 2), TOKEN_AXES)
    by_token = P(TOKEN_AXES, None)
    by_row = P("fs", None)
    return jax.shard_map(
        shards,
        mesh=fine,
        in_specs=(by_token,) + (P(),) * 7 + (by_row,) * 5 + (by_token,),
        out_specs=(by_token, by_token) + (P(),) * 7 + (by_token,) * 5,
        check_vma=False,
    )
```

```python
import math

import jax
import jax.numpy as jnp
from jax import lax
from jax.experimental import pallas as pl
from jax.experimental.pallas import tpu as pltpu
from jax.sharding import Mesh
from jax.sharding import PartitionSpec as P

HP = 64
NS = 128
KW = 4
SBLK = 256
MASKED = -1e30
HIGHEST = lax.Precision.HIGHEST
F32 = jnp.float32
BF16 = jnp.bfloat16
VMEM_LIMIT = 56 * 1024 * 1024
XW = 192
CW = 448
HALO = 16
DT_AT = 640
Q_AT = 448
KV_AT = 512


def nn(a, b, precision=None):
    return lax.dot_general(
        a, b, (((1,), (0,)), ((), ())), precision=precision, preferred_element_type=F32
    )


def nt(a, b):
    return lax.dot_general(a, b, (((1,), (1,)), ((), ())), preferred_element_type=F32)


def tn(a, b):
    return lax.dot_general(a, b, (((0,), (0,)), ((), ())), preferred_element_type=F32)


def iota(shape, dim):
    return lax.broadcasted_iota(jnp.int32, shape, dim)


def spread(per_head, rows):
    return jnp.concatenate(
        [jnp.broadcast_to(per_head[:, h : h + 1], (rows, HP)) for h in range(XW // HP)], axis=1
    )


def head_sum_matrix():
    return (iota((XW, 128), 0) // HP == iota((XW, 128), 1)).astype(F32)


def conv_pre(ext, weights, base, lanes=slice(None)):
    pre = ext[pl.ds(base + HALO - 3, SBLK), :] * weights[0:1, :]
    for k in range(1, KW):
        pre = pre + ext[pl.ds(base + HALO - 3 + k, SBLK), :] * weights[k : k + 1, :]
    return pre


def step_and_log(slab, par_ref, base):
    raw = slab[pl.ds(base, SBLK), DT_AT:].astype(F32) + par_ref[1:2, :]
    step = jnp.maximum(raw, 0.0) + jnp.log1p(jnp.exp(-jnp.abs(raw)))
    return raw, step, -jnp.exp(par_ref[0:1, :]) * step


def ssd_forward(slab, halo, taps, par, y_out, state_out, c_out, cum_out, entry_out, ext):
    length = slab.shape[0]
    ext[pl.ds(0, HALO), :] = halo[...].astype(F32)
    ext[pl.ds(HALO, length), :] = slab[:, :CW].astype(F32)
    weights = taps[...]
    lower = iota((SBLK, SBLK), 0) >= iota((SBLK, SBLK), 1)
    tri = lower.astype(F32)
    state_out[...] = jnp.zeros_like(state_out)
    before = jnp.zeros((1, 128), F32)
    for k in range(length // SBLK):
        base = k * SBLK
        pre = conv_pre(ext, weights, base)
        conv = pre * jax.nn.sigmoid(pre)
        b_low = conv[:, :NS].astype(BF16)
        c_low = conv[:, NS : 2 * NS].astype(BF16)
        x = conv[:, 2 * NS :]
        raw, step, log = step_and_log(slab, par, base)
        cum = nn(tri, log, HIGHEST)
        cum_t = cum.T
        u = x * spread(step, SBLK)
        u_low = u.astype(BF16)
        inner = nt(c_low, b_low)
        state = state_out[pl.ds(0, XW), :]
        entry_out[k] = state
        parts = []
        for h in range(XW // HP):
            decay = jnp.exp(
                jnp.where(lower, cum[:, h : h + 1] - cum_t[h : h + 1, :], MASKED)
            )
            parts.append(nn((inner * decay).astype(BF16), u_low[:, h * HP : (h + 1) * HP]))
        carried = nt(c_low, state.astype(BF16)) * spread(jnp.exp(cum), SBLK)
        y_out[pl.ds(base, SBLK), :] = (
            jnp.concatenate(parts, axis=1) + carried + spread(par[2:3, :], 1) * x
        )
        last = cum[SBLK - 1 : SBLK, :]
        tail = (u * spread(jnp.exp(last - cum), SBLK)).astype(BF16)
        shrink = jnp.concatenate(
            [
                jnp.broadcast_to(jnp.exp(last[:, h : h + 1]), (HP, NS))
                for h in range(XW // HP)
            ],
            axis=0,
        )
        state_out[pl.ds(0, XW), :] = state * shrink + tn(tail, b_low)
        c_out[pl.ds(base, SBLK), :] = c_low
        cum_out[pl.ds(base, SBLK), :] = cum + before
        before = before + last
    state_out[pl.ds(XW, 8), :] = jnp.broadcast_to(before, (8, 128))


def ssd_forward_call(slab, halo, taps, par):
    length = slab.shape[0]
    return pl.pallas_call(
        ssd_forward,
        out_shape=(
            jax.ShapeDtypeStruct((length, XW), F32),
            jax.ShapeDtypeStruct((XW + 8, NS), F32),
            jax.ShapeDtypeStruct((length, NS), BF16),
            jax.ShapeDtypeStruct((length, 128), F32),
            jax.ShapeDtypeStruct((length // SBLK, XW, NS), F32),
        ),
        scratch_shapes=[pltpu.VMEM((length + HALO, CW), F32)],
        compiler_params=pltpu.CompilerParams(vmem_limit_bytes=VMEM_LIMIT),
        cost_estimate=pl.CostEstimate(
            flops=8_000_000_000, bytes_accessed=8_000_000, transcendentals=1_000_000
        ),
        name="ssd_forward",
    )(slab, halo, taps, par)


def shrink_rows(log_row):
    return jnp.concatenate(
        [jnp.broadcast_to(jnp.exp(log_row[:, h : h + 1]), (HP, NS)) for h in range(XW // HP)],
        axis=0,
    )


def ssd_join(y, c, cum, near, mid, far, attended, out, entering):
    state = near[pl.ds(0, XW), :] + shrink_rows(near[XW : XW + 1, :]) * (
        mid[pl.ds(0, XW), :] + shrink_rows(mid[XW : XW + 1, :]) * far[pl.ds(0, XW), :]
    )
    entering[...] = state
    state_low = state.astype(BF16)
    rows = y.shape[0]
    for base in range(0, rows, SBLK):
        at = pl.ds(base, SBLK)
        mixed = y[at, :] + nt(c[at, :], state_low) * spread(jnp.exp(cum[at, :]), SBLK)
        out[at, :] = jnp.concatenate([mixed, attended[at, :]], axis=1).astype(BF16)


def ssd_join_call(y, c, cum, near, mid, far, attended):
    return pl.pallas_call(
        ssd_join,
        out_shape=(
            jax.ShapeDtypeStruct((y.shape[0], XW + HP), BF16),
            jax.ShapeDtypeStruct((XW, NS), F32),
        ),
        compiler_params=pltpu.CompilerParams(vmem_limit_bytes=VMEM_LIMIT),
        name="ssd_join",
    )(y, c, cum, near, mid, far, attended)


def ssd_entry_gradient(grad, c, cum, out):
    rows = grad.shape[0]
    total = jnp.zeros((XW, NS), F32)
    for base in range(0, rows, SBLK):
        at = pl.ds(base, SBLK)
        scaled = grad[at, :XW].astype(F32) * spread(jnp.exp(cum[at, :]), SBLK)
        total = total + tn(scaled.astype(BF16), c[at, :])
    out[pl.ds(0, XW), :] = total
    out[pl.ds(XW, 8), :] = jnp.broadcast_to(cum[rows - 1 : rows, :], (8, 128))


def ssd_entry_gradient_call(grad, c, cum):
    return pl.pallas_call(
        ssd_entry_gradient,
        out_shape=jax.ShapeDtypeStruct((XW + 8, NS), F32),
        compiler_params=pltpu.CompilerParams(vmem_limit_bytes=VMEM_LIMIT),
        name="ssd_entry_gradient",
    )(grad, c, cum)


def ssd_backward(
    slab, halo, taps, par, grad, entry, cum_all, entering, near, mid, far,
    grad_in, grad_dt, grad_rim, grad_taps, grad_par, ext, gpre,
):
    length = slab.shape[0]
    chunks = length // SBLK
    ext[pl.ds(0, HALO), :] = halo[...].astype(F32)
    ext[pl.ds(HALO, length), :] = slab[:, :CW].astype(F32)
    gpre[pl.ds(length, HALO), :] = jnp.zeros((HALO, CW), F32)
    weights = taps[...]
    lower = iota((SBLK, SBLK), 0) >= iota((SBLK, SBLK), 1)
    tri = lower.astype(F32)
    upper = (iota((SBLK, SBLK), 0) <= iota((SBLK, SBLK), 1)).astype(F32)
    hsum = head_sum_matrix()
    rate = jnp.exp(par[0:1, :])
    skip = spread(par[2:3, :], 1)
    enter = entering[...]
    later = near[pl.ds(0, XW), :] + shrink_rows(near[XW : XW + 1, :]) * (
        mid[pl.ds(0, XW), :] + shrink_rows(mid[XW : XW + 1, :]) * far[pl.ds(0, XW), :]
    )
    g_decay = jnp.zeros((1, 128), F32)
    g_bias = jnp.zeros((1, 128), F32)
    g_skip = jnp.zeros((1, 128), F32)
    for k in reversed(range(chunks)):
        base = k * SBLK
        at = pl.ds(base, SBLK)
        pre = conv_pre(ext, weights, base)
        sig = jax.nn.sigmoid(pre)
        conv = pre * sig
        b_low = conv[:, :NS].astype(BF16)
        c_low = conv[:, NS : 2 * NS].astype(BF16)
        x = conv[:, 2 * NS :]
        raw, step, log = step_and_log(slab, par, base)
        cum = nn(tri, log, HIGHEST)
        cum_t = cum.T
        last = cum[SBLK - 1 : SBLK, :]
        step_wide = spread(step, SBLK)
        u_low = (x * step_wide).astype(BF16)
        u = u_low.astype(F32)
        gy_low = grad[at, :XW]
        gy = gy_low.astype(F32)
        if k:
            state = entry[k] + shrink_rows(cum_all[base - 1 : base, :]) * enter
        else:
            state = enter
        state_low = state.astype(BF16)
        later_low = later.astype(BF16)
        inner = nt(c_low, b_low)
        g_inner = jnp.zeros((SBLK, SBLK), F32)
        y_parts, gu_parts = [], []
        for h in range(XW // HP):
            lanes = slice(h * HP, (h + 1) * HP)
            decay = jnp.exp(
                jnp.where(lower, cum[:, h : h + 1] - cum_t[h : h + 1, :], MASKED)
            )
            kernel = (inner * decay).astype(BF16)
            y_parts.append(nn(kernel, u_low[:, lanes]))
            gu_parts.append(tn(kernel, gy_low[:, lanes]))
            g_inner = g_inner + nt(gy_low[:, lanes], u_low[:, lanes]) * decay
        g_inner_low = g_inner.astype(BF16)
        enter_wide = spread(jnp.exp(cum), SBLK)
        tail_wide = spread(jnp.exp(last - cum), SBLK)
        gy_scaled = (gy * enter_wide).astype(BF16)
        u_scaled = (u * tail_wide).astype(BF16)
        y = jnp.concatenate(y_parts, axis=1) + nt(c_low, state_low) * enter_wide
        tail = nt(b_low, later_low) * tail_wide
        gu = jnp.concatenate(gu_parts, axis=1) + tail
        gc = nn(g_inner_low, b_low) + nn(gy_scaled, state_low)
        gb = tn(g_inner_low, c_low) + nn(u_scaled, later_low)
        shrink = shrink_rows(last)
        both = nn(gy * y - u * gu, hsum, HIGHEST)
        tail_sum = jnp.sum(nn(u * tail, hsum, HIGHEST), axis=0, keepdims=True)
        across = jnp.sum(
            jnp.sum(later * state * shrink, axis=1, keepdims=True) * hsum, axis=0, keepdims=True
        )
        g_log = nn(upper, both, HIGHEST) + tail_sum + across
        g_step = nn(x * gu, hsum, HIGHEST) - rate * g_log
        g_raw = g_step * jax.nn.sigmoid(raw)
        g_decay = g_decay + jnp.sum(g_log * log, axis=0, keepdims=True)
        g_bias = g_bias + jnp.sum(g_raw, axis=0, keepdims=True)
        g_skip = g_skip + jnp.sum(nn(gy * x, hsum, HIGHEST), axis=0, keepdims=True)
        grad_dt[at, :] = g_raw
        g_conv = jnp.concatenate([gb, gc, step_wide * gu + skip * gy], axis=1)
        gpre[at, :] = g_conv * (sig + conv * (1.0 - sig))
        later = shrink * later + tn(gy_scaled, c_low)
    for k in range(chunks):
        base = k * SBLK
        acc = gpre[pl.ds(base + 3, SBLK), :] * weights[0:1, :]
        for tap in range(1, KW):
            acc = acc + gpre[pl.ds(base + 3 - tap, SBLK), :] * weights[tap : tap + 1, :]
        grad_in[pl.ds(base, SBLK), :] = acc
    first = gpre[pl.ds(0, 8), :]
    rim = jnp.zeros((8, CW), F32)
    rows = iota((8, CW), 0)
    for back in range(1, KW):
        term = jnp.zeros((1, CW), F32)
        for tap in range(KW):
            t = 3 - tap - back
            if 0 <= t:
                term = term + first[t : t + 1, :] * weights[tap : tap + 1, :]
        rim = jnp.where(rows == 8 - back, term, rim)
    grad_rim[...] = rim
    g_taps = jnp.zeros((8, CW), F32)
    rows = iota((8, CW), 0)
    for tap in range(KW):
        total = jnp.zeros((1, CW), F32)
        for k in range(chunks):
            base = k * SBLK
            total = total + jnp.sum(
                gpre[pl.ds(base, SBLK), :] * ext[pl.ds(base + HALO - 3 + tap, SBLK), :],
                axis=0,
                keepdims=True,
            )
        g_taps = jnp.where(rows == tap, total, g_taps)
    grad_taps[...] = g_taps
    rows = iota((8, 128), 0)
    grad_par[...] = jnp.where(
        rows == 0, g_decay, jnp.where(rows == 1, g_bias, jnp.where(rows == 2, g_skip, 0.0))
    )


def ssd_backward_call(slab, halo, taps, par, grad, entry, cum, entering, near, mid, far):
    length = slab.shape[0]
    return pl.pallas_call(
        ssd_backward,
        out_shape=(
            jax.ShapeDtypeStruct((length, CW), F32),
            jax.ShapeDtypeStruct((length, 128), F32),
            jax.ShapeDtypeStruct((8, CW), F32),
            jax.ShapeDtypeStruct((8, CW), F32),
            jax.ShapeDtypeStruct((8, 128), F32),
        ),
        scratch_shapes=[
            pltpu.VMEM((length + HALO, CW), F32),
            pltpu.VMEM((length + HALO, CW), F32),
        ],
        compiler_params=pltpu.CompilerParams(vmem_limit_bytes=VMEM_LIMIT),
        cost_estimate=pl.CostEstimate(
            flops=20_000_000_000, bytes_accessed=12_000_000, transcendentals=2_000_000
        ),
        name="ssd_backward",
    )(slab, halo, taps, par, grad, entry, cum, entering, near, mid, far)


QB = 256
KB = 512


def place_keys(rank, parts, kv):
    length = parts[0].shape[0]
    for back, part in enumerate(parts):

        @pl.when(rank >= back)
        def _():
            kv[pl.ds(pl.multiple_of((rank - back) * length, length), length), :] = part[...]


def attend_forward(rank_ref, slab, near, mid, far, out, lse, kv, own):
    length = slab.shape[0]
    rank = rank_ref[0]
    offset = rank * length
    scale = HP**-0.5
    ahead = iota((QB, KB), 0) - iota((QB, KB), 1)
    own[...] = slab[:, KV_AT:DT_AT]
    place_keys(rank, (own, near, mid, far), kv)

    def q_step(i, _):
        at = pl.ds(pl.multiple_of(i * QB, QB), QB)
        q_blk = (slab[at, Q_AT:KV_AT].astype(F32) * scale).astype(BF16)
        first = offset + i * QB

        def block(j, carry, masked):
            top, total, acc = carry
            at = pl.ds(pl.multiple_of(j * KB, KB), KB)
            s = nt(q_blk, kv[at, :HP])
            if masked:
                s = jnp.where(ahead >= j * KB - first, s, MASKED)
            new = jnp.maximum(top, jnp.max(s, axis=1, keepdims=True))
            p = jnp.exp(s - new)
            fade = jnp.exp(top - new)
            total = total * fade + jnp.sum(p, axis=1, keepdims=True)
            acc = acc * fade + nn(p.astype(BF16), kv[at, HP:])
            return new, total, acc

        whole = first // KB
        carry = (
            jnp.full((QB, 1), MASKED, F32),
            jnp.zeros((QB, 1), F32),
            jnp.zeros((QB, HP), F32),
        )
        carry = lax.fori_loop(0, whole, lambda j, c: block(j, c, False), carry)
        top, total, acc = block(whole, carry, True)
        out[at, :] = acc / total
        lse[at, :] = jnp.broadcast_to(top + jnp.log(total), (QB, 128))
        return 0

    lax.fori_loop(0, length // QB, q_step, 0)


def attend_forward_call(rank, slab, near, mid, far):
    length = slab.shape[0]
    vm = pl.BlockSpec(memory_space=pltpu.VMEM)
    return pl.pallas_call(
        attend_forward,
        in_specs=[pl.BlockSpec(memory_space=pltpu.SMEM)] + [vm] * 4,
        out_shape=(
            jax.ShapeDtypeStruct((length, HP), F32),
            jax.ShapeDtypeStruct((length, 128), F32),
        ),
        scratch_shapes=[
            pltpu.VMEM((4 * length, 2 * HP), BF16),
            pltpu.VMEM((length, 2 * HP), BF16),
        ],
        compiler_params=pltpu.CompilerParams(vmem_limit_bytes=VMEM_LIMIT),
        cost_estimate=pl.CostEstimate(
            flops=8_000_000_000, bytes_accessed=4_000_000, transcendentals=4_000_000
        ),
        name="attend_forward",
    )(rank, slab, near, mid, far)


def attend_backward(
    rank_ref, slab, near, mid, far, g, out, lse, gq, g_own, g_near, g_mid, g_far, kv, own, acc
):
    length = slab.shape[0]
    rank = rank_ref[0]
    offset = rank * length
    scale = HP**-0.5
    ahead = iota((QB, KB), 0) - iota((QB, KB), 1)
    own[...] = slab[:, KV_AT:DT_AT]
    place_keys(rank, (own, near, mid, far), kv)
    acc[...] = jnp.zeros_like(acc)

    def q_step(i, _):
        at_q = pl.ds(pl.multiple_of(i * QB, QB), QB)
        q_blk = (slab[at_q, Q_AT:KV_AT].astype(F32) * scale).astype(BF16)
        g_low = g[at_q, XW:]
        delta = jnp.sum(g_low.astype(F32) * out[at_q, :], axis=1, keepdims=True)
        log_total = lse[at_q, 0:1]
        first = offset + i * QB

        def block(j, gq_acc, masked):
            at = pl.ds(pl.multiple_of(j * KB, KB), KB)
            k_blk = kv[at, :HP]
            s = nt(q_blk, k_blk)
            if masked:
                s = jnp.where(ahead >= j * KB - first, s, MASKED)
            p = jnp.exp(s - log_total)
            dp = nt(g_low, kv[at, HP:])
            ds = (p * (dp - delta)).astype(BF16)
            acc[at, :] += jnp.concatenate([tn(ds, q_blk), tn(p.astype(BF16), g_low)], axis=1)
            return gq_acc + nn(ds, k_blk)

        whole = first // KB
        carry = jnp.zeros((QB, HP), F32)
        carry = lax.fori_loop(0, whole, lambda j, c: block(j, c, False), carry)
        gq[at_q, :] = block(whole, carry, True) * scale
        return 0

    lax.fori_loop(0, length // QB, q_step, 0)
    for back, target in enumerate((g_own, g_near, g_mid, g_far)):

        @pl.when(rank >= back)
        def _():
            at = pl.ds(pl.multiple_of((rank - back) * length, length), length)
            target[...] = acc[at, :].astype(target.dtype)

        @pl.when(rank < back)
        def _():
            target[...] = jnp.zeros_like(target)


def attend_backward_call(rank, slab, near, mid, far, g, out, lse):
    length = slab.shape[0]
    vm = pl.BlockSpec(memory_space=pltpu.VMEM)
    keys = jax.ShapeDtypeStruct((length, 2 * HP), BF16)
    return pl.pallas_call(
        attend_backward,
        in_specs=[pl.BlockSpec(memory_space=pltpu.SMEM)] + [vm] * 7,
        out_shape=(
            jax.ShapeDtypeStruct((length, HP), F32),
            jax.ShapeDtypeStruct((length, 2 * HP), F32),
            keys,
            keys,
            keys,
        ),
        scratch_shapes=[
            pltpu.VMEM((4 * length, 2 * HP), BF16),
            pltpu.VMEM((length, 2 * HP), BF16),
            pltpu.VMEM((4 * length, 2 * HP), F32),
        ],
        compiler_params=pltpu.CompilerParams(vmem_limit_bytes=VMEM_LIMIT),
        cost_estimate=pl.CostEstimate(
            flops=20_000_000_000, bytes_accessed=4_000_000, transcendentals=4_000_000
        ),
        name="attend_backward",
    )(rank, slab, near, mid, far, g, out, lse)


CORE_ROWS = 16
PARTS = (0, 768, 1536, 2176)
ORDERS = ((0, 1, 2), (1, 2, 0), (2, 0, 1))
TORUS = ("fs", "cp", "ux")


def sum_over_devices(
    left, right, small, out, small_out,
    left_in, right_in, part0, part1, part2, got10, got11, got12, mid0, mid1, mid2,
    got20, got21, got22, end0, end1, end2, got30, got31, got32, done, done_in, small_in, small_core,
    core_send, core_recv, send, recv, small_send, small_recv,
):
    mesh_kind = pl.DeviceIdType.MESH
    core = lax.axis_index("uc")
    place = [lax.axis_index(a) for a in TORUS]
    other = {"uc": 1 - core}
    half = right.shape[1] // 2
    rows = left.shape[0]

    def peer(axis, shift):
        return {TORUS[axis]: lax.rem(place[axis] + shift, 4)}

    barrier = pltpu.get_barrier_semaphore()
    pl.semaphore_signal(barrier, inc=1, device_id=other, device_id_type=mesh_kind)
    for axis in range(3):
        for shift in (1, 2, 3):
            pl.semaphore_signal(
                barrier, inc=1, device_id=peer(axis, shift), device_id_type=mesh_kind
            )
    pl.semaphore_wait(barrier, 10)

    def remote(src, dst, send_sem, recv_sem, target):
        copy = pltpu.make_async_remote_copy(
            src_ref=src, dst_ref=dst, send_sem=send_sem, recv_sem=recv_sem,
            device_id=target, device_id_type=mesh_kind,
        )
        copy.start()
        return copy

    theirs = pl.ds(pl.multiple_of((1 - core) * half, 128), half)
    ours = pl.ds(pl.multiple_of(core * half, 128), half)
    core_copies = [
        remote(left, left_in, core_send.at[0], core_recv.at[0], other),
        remote(right.at[:, theirs], right_in, core_send.at[1], core_recv.at[1], other),
        remote(small, small_core, core_send.at[2], core_recv.at[2], other),
    ]
    for copy in core_copies:
        copy.wait()

    parts = (part0, part1, part2)
    got1, got2, got3 = (got10, got11, got12), (got20, got21, got22), (got30, got31, got32)
    mids, ends = (mid0, mid1, mid2), (end0, end1, end2)
    lefts = [(left[:, f * 256 : (f + 1) * 256], left_in[:, f * 256 : (f + 1) * 256]) for f in range(4)]
    first = []
    for p in range(3):
        width = PARTS[p + 1] - PARTS[p]
        at = pl.ds(pl.multiple_of(core * half + PARTS[p], 128), width)
        mine, their = right[:, at], right_in[:, PARTS[p] : PARTS[p + 1]]
        rights = jnp.concatenate([mine, their], axis=0)
        for f in range(4):
            block = tn(jnp.concatenate(lefts[f], axis=0), rights).astype(BF16)
            for c in range(4):
                for x in range(4):
                    where = (f, c, x)
                    a0, a1, a2 = (where[a] for a in ORDERS[p])
                    start = (c * 4 + x) * CORE_ROWS
                    parts[p][a0, a1, a2] = block[start : start + CORE_ROWS]
        axis = ORDERS[p][0]
        first.append(
            [
                remote(
                    parts[p].at[lax.rem(place[axis] + shift, 4)], got1[p].at[shift - 1],
                    send.at[p, 0, shift - 1], recv.at[p, 0, shift - 1], peer(axis, shift),
                )
                for shift in (1, 2, 3)
            ]
        )

    total = small[...] + small_core[...]
    for axis in range(3):
        small_in[axis, place[axis]] = total
        copies = [
            remote(
                small_in.at[axis, place[axis]], small_in.at[axis, place[axis]],
                small_send.at[axis, shift - 1], small_recv.at[axis, shift - 1], peer(axis, shift),
            )
            for shift in (1, 2, 3)
        ]
        for copy in copies:
            copy.wait()
        total = (small_in[axis, 0] + small_in[axis, 1]) + (small_in[axis, 2] + small_in[axis, 3])
    small_out[...] = total

    def add(source, slots, index):
        acc = source[index].astype(F32)
        for s in range(3):
            acc = acc + slots[s].astype(F32)
        return acc

    second = []
    for p in range(3):
        for copy in first[p]:
            copy.wait()
        for i in range(4):
            acc = parts[p][place[ORDERS[p][0]], i].astype(F32)
            for s in range(3):
                acc = acc + got1[p][s, i].astype(F32)
            mids[p][i] = acc.astype(BF16)
        axis = ORDERS[p][1]
        second.append(
            [
                remote(
                    mids[p].at[lax.rem(place[axis] + shift, 4)], got2[p].at[shift - 1],
                    send.at[p, 1, shift - 1], recv.at[p, 1, shift - 1], peer(axis, shift),
                )
                for shift in (1, 2, 3)
            ]
        )
    third = []
    for p in range(3):
        for copy in second[p]:
            copy.wait()
        ends[p][...] = add(mids[p], got2[p], place[ORDERS[p][1]]).astype(BF16)
        axis = ORDERS[p][2]
        third.append(
            [
                remote(
                    ends[p].at[lax.rem(place[axis] + shift, 4)], got3[p].at[shift - 1],
                    send.at[p, 2, shift - 1], recv.at[p, 2, shift - 1], peer(axis, shift),
                )
                for shift in (1, 2, 3)
            ]
        )
    for p in range(3):
        for copy in third[p]:
            copy.wait()
        done[:, PARTS[p] : PARTS[p + 1]] = add(ends[p], got3[p], place[ORDERS[p][2]])
    keep = pl.ds(pl.multiple_of(core * 8, 8), 8)
    give = pl.ds(pl.multiple_of((1 - core) * 8, 8), 8)
    last = remote(done.at[give, :], done_in, core_send.at[3], core_recv.at[3], other)
    out[:, ours] = done[keep, :]
    last.wait()
    out[:, theirs] = done_in[...]


def sum_over_devices_call(left, right, small):
    half = right.shape[1] // 2
    widths = [PARTS[p + 1] - PARTS[p] for p in range(3)]

    def blocks(*lead):
        return [pltpu.VMEM(lead + (CORE_ROWS, w), BF16) for w in widths]

    return pl.pallas_call(
        sum_over_devices,
        in_specs=[pl.BlockSpec(memory_space=pltpu.VMEM)] * 3,
        out_specs=[pl.BlockSpec(memory_space=pltpu.VMEM)] * 2,
        out_shape=(
            jax.ShapeDtypeStruct((8, 2 * half), F32),
            jax.ShapeDtypeStruct(small.shape, F32),
        ),
        scratch_shapes=[
            pltpu.VMEM(left.shape, BF16),
            pltpu.VMEM((left.shape[0], half), BF16),
            *blocks(4, 4, 4),
            *blocks(3, 4, 4),
            *blocks(4, 4),
            *blocks(3, 4),
            *blocks(4),
            *blocks(3),
            pltpu.VMEM((CORE_ROWS, half), F32),
            pltpu.VMEM((8, half), F32),
            pltpu.VMEM((3, 4) + small.shape, F32),
            pltpu.VMEM(small.shape, F32),
            pltpu.SemaphoreType.DMA((4,)),
            pltpu.SemaphoreType.DMA((4,)),
            pltpu.SemaphoreType.DMA((3, 3, 3)),
            pltpu.SemaphoreType.DMA((3, 3, 3)),
            pltpu.SemaphoreType.DMA((3, 3)),
            pltpu.SemaphoreType.DMA((3, 3)),
        ],
        compiler_params=pltpu.CompilerParams(
            vmem_limit_bytes=VMEM_LIMIT, collective_id=0, has_side_effects=True
        ),
        cost_estimate=pl.CostEstimate(
            flops=1_200_000_000, bytes_accessed=4_000_000, transcendentals=0
        ),
        name="sum_over_devices",
    )(left, right, small)


HM = 24
GROUPS = 8
HEADS = 8
KEY_HEADS = 2
FF = 2048
DS = 1536
PROJ = 4120
PROJ_WIDE = 4352
EPSILON = 1e-05
TOKEN_AXES = ("fs", "cp", "ux", "uc")


def rms_norm(values, norm_gain):
    return (
        values * lax.rsqrt(jnp.mean(values * values, axis=-1, keepdims=True) + EPSILON) * norm_gain
    )


def gated_norm(mixed_heads, gate_pre, norm_gain):
    return rms_norm(mixed_heads * jax.nn.silu(gate_pre), norm_gain)


def from_behind(block, distance):
    return lax.ppermute(block, "cp", [(i - distance, i) for i in range(distance, 4)])


def from_ahead(block, distance):
    return lax.ppermute(block, "cp", [(i, i - distance) for i in range(distance, 4)])


def other_core(block):
    return lax.ppermute(block, "uc", [(0, 1), (1, 0)])


def columns_half(block, half):
    width = block.shape[1] // 2
    return lax.dynamic_slice_in_dim(block, half * width, width, 1)


def gather_half(shard, core):
    rows = shard.shape[0] // 2
    mine = lax.dynamic_slice_in_dim(shard, core * rows, rows, 0)
    return lax.all_gather(mine, "fs", axis=0, tiled=True)


def both_cores(left, right, core):
    lefts = jnp.concatenate([left, other_core(left)], axis=0)
    rights = jnp.concatenate(
        [columns_half(right, core), other_core(columns_half(right, 1 - core))], axis=0
    )
    return lefts, rights


def core_halves(rows, core):
    r = rows.shape[0] // 2
    mine = lax.dynamic_slice_in_dim(rows, core * r, r, 0)
    theirs = other_core(lax.dynamic_slice_in_dim(rows, (1 - core) * r, r, 0))
    return jnp.concatenate(
        [jnp.where(core == 0, mine, theirs), jnp.where(core == 0, theirs, mine)], axis=1
    ).astype(F32)


def weight_products(pairs, core):
    blocks = []
    for left, right in pairs:
        lefts, rights = both_cores(left, right, core)
        for at in range(0, rights.shape[1], 512):
            part = tn(lefts, rights[:, at : at + 512]).astype(BF16)
            blocks.append(part.reshape(64, part.shape[0] // 64, 512))
    return jnp.concatenate(blocks, axis=1)


def split_products(total, pairs, core):
    results, at = [], 0
    for left, right in pairs:
        r = left.shape[1] // 64
        count = right.shape[1] // 1024
        whole = jnp.concatenate(
            [total[at + i * r : at + (i + 1) * r] for i in range(count)], axis=1
        )
        at += count * r
        results.append(core_halves(whole, core))
    return results


def scatter_sum(total, axis):
    return lax.psum_scatter(total, axis, scatter_dimension=0, tiled=True)


def shards(
    tokens,
    norm_in,
    norm_mid,
    mamba_gain,
    conv_weight,
    decay_log,
    dt_bias,
    skip_gain,
    w_in,
    w_mout,
    w_aout,
    w_gu,
    w_down,
    grad_out,
):
    part_rank = lax.axis_index("cp")
    core = lax.axis_index("uc")
    group = lax.axis_index("ux") * 2 + core
    rows = tokens.shape[0]
    length = GROUPS * rows
    heads = HM // GROUPS
    in_ours = gather_half(w_in, core)
    in_theirs = other_core(in_ours)
    mout_ours = gather_half(w_mout, core)
    full_aout = lax.all_gather(w_aout, "fs", axis=0, tiled=True)
    gu_ours = gather_half(w_gu, core)
    down_ours = gather_half(w_down, core)

    def halves(block):
        pieces = block.reshape(rows, 4, 2, block.shape[1] // 8)
        picked = [
            lax.dynamic_index_in_dim(pieces, which, 2, False).reshape(rows, block.shape[1] // 2)
            for which in (core, 1 - core)
        ]
        return picked

    def times_halves(block, ours, theirs):
        own, rest = halves(block)
        return nn(own, ours) + nn(rest, theirs)

    def times_halves_transposed(block, ours, theirs):
        own = nt(block, ours).reshape(rows, 4, -1)
        rest = nt(block, theirs).reshape(rows, 4, -1)
        pieces = jnp.where(core == 0, jnp.stack([own, rest], 2), jnp.stack([rest, own], 2))
        return pieces.reshape(rows, -1)

    def to_groups(blocks):
        return lax.all_to_all(blocks, ("ux", "uc"), split_axis=0, concat_axis=0, tiled=True)

    resid_in = tokens.astype(F32)
    normed_f, in_back = jax.vjp(rms_norm, resid_in, norm_in)
    normed_in = normed_f.astype(BF16)
    projected = times_halves(normed_in, in_ours, in_theirs)
    gate_pre = projected[:, :DS]
    low = projected[:, DS:].astype(BF16)
    q_at = DS + 2 * NS + HM
    k_at = q_at + HEADS * HP
    v_at = k_at + KEY_HEADS * HP
    blocks = []
    for g in range(GROUPS):
        key = g * KEY_HEADS // GROUPS
        blocks.append(
            jnp.concatenate(
                [
                    low[:, DS : DS + 2 * NS],
                    low[:, g * XW : (g + 1) * XW],
                    low[:, q_at + g * HP : q_at + (g + 1) * HP],
                    low[:, k_at + key * HP : k_at + (key + 1) * HP],
                    low[:, v_at + key * HP : v_at + (key + 1) * HP],
                    low[:, DS + 2 * NS + g * heads : DS + 2 * NS + (g + 1) * heads],
                    jnp.zeros((rows, 128 - heads), BF16),
                ],
                axis=1,
            )
        )
    slab = to_groups(jnp.stack(blocks)).reshape(length, DT_AT + 128)

    taps = jnp.concatenate(
        [conv_weight[:, DS:], lax.dynamic_slice_in_dim(conv_weight, group * XW, XW, 1)], axis=1
    )
    taps = jnp.pad(taps, ((0, 8 - KW), (0, 0)))
    per_head = jnp.stack([decay_log, dt_bias, skip_gain])
    par = jnp.pad(
        lax.dynamic_slice_in_dim(per_head, group * heads, heads, 1), ((0, 5), (0, 128 - heads))
    )
    rank = part_rank.astype(jnp.int32).reshape(1)

    halo = from_behind(slab[length - HALO :, :CW], 1)
    own_keys = slab[:, KV_AT:DT_AT]
    keys = [from_behind(own_keys, d) for d in (1, 2, 3)]
    y, state, c_low, cum, entry = ssd_forward_call(slab, halo, taps, par)
    mout_ours, y = lax.optimization_barrier((mout_ours, y))
    mout_theirs = other_core(mout_ours)
    states = [from_behind(state, d) for d in (1, 2, 3)]
    attended, lse = attend_forward_call(rank, slab, *keys)
    gu_ours, attended = lax.optimization_barrier((gu_ours, attended))
    gu_theirs = other_core(gu_ours)
    joined, entering = ssd_join_call(y, c_low, cum, *states, attended)
    tok = to_groups(joined.reshape(GROUPS, rows, XW + HP)).transpose(1, 0, 2)
    down_ours, tok = lax.optimization_barrier((down_ours, tok))
    down_theirs = other_core(down_ours)
    mixed_tok = tok[:, :, :XW].reshape(rows, DS)
    attended_tok = tok[:, :, XW:].reshape(rows, HEADS * HP)

    branch_f, gate_back = jax.vjp(gated_norm, mixed_tok.astype(F32), gate_pre, mamba_gain)
    branch_low = branch_f.astype(BF16)
    resid_mid = resid_in + times_halves(branch_low, mout_ours, mout_theirs) + nn(attended_tok, full_aout)
    normed_mid_f, mid_back = jax.vjp(rms_norm, resid_mid, norm_mid)
    normed_mid = normed_mid_f.astype(BF16)
    gate_up = times_halves(normed_mid, gu_ours, gu_theirs)
    gate_half = gate_up[:, :FF]
    up_half = gate_up[:, FF:]
    sigmoid_gate = jax.nn.sigmoid(gate_half)
    hidden = (gate_half * sigmoid_gate * up_half).astype(BF16)
    layer_out = (resid_mid + times_halves(hidden, down_ours, down_theirs)).astype(BF16)
    grad_hidden = times_halves_transposed(grad_out, down_ours, down_theirs)
    grad_gate = grad_hidden * up_half * sigmoid_gate * (1.0 + gate_half * (1.0 - sigmoid_gate))
    grad_up = grad_hidden * gate_half * sigmoid_gate
    grad_gate_up = jnp.concatenate([grad_gate, grad_up], axis=1).astype(BF16)
    resid_back, grad_norm_mid = mid_back(
        times_halves_transposed(grad_gate_up, gu_ours, gu_theirs)
    )
    grad_resid = grad_out.astype(F32) + resid_back
    resid_low = grad_resid.astype(BF16)
    grad_mixed, grad_gate_pre, grad_mamba_gain = gate_back(
        times_halves_transposed(resid_low, mout_ours, mout_theirs)
    )
    grad_attended = nt(resid_low, full_aout)
    grad_blocks = jnp.concatenate(
        [
            grad_mixed.astype(BF16).reshape(rows, GROUPS, XW),
            grad_attended.astype(BF16).reshape(rows, GROUPS, HP),
        ],
        axis=2,
    ).transpose(1, 0, 2)
    grad = to_groups(grad_blocks).reshape(length, XW + HP)
    pairs = [
        (normed_mid, grad_gate_up),
        (hidden, grad_out),
        (branch_low, resid_low),
        (attended_tok, resid_low),
    ]
    total = scatter_sum(weight_products(pairs, core), "fs")

    entry_gradient = ssd_entry_gradient_call(grad, c_low, cum)
    later = [from_ahead(entry_gradient, d) for d in (1, 2, 3)]
    grad_query, key_own, *key_parts = attend_backward_call(rank, slab, *keys, grad, attended, lse)
    key_parts = [from_ahead(p, d + 1) for d, p in enumerate(key_parts)]
    grad_in_cols, grad_dt, rim, grad_taps, grad_par = ssd_backward_call(
        slab, halo, taps, par, grad, entry, cum, entering, *later
    )
    rim = from_ahead(rim, 1)
    total, rim, grad_query = lax.optimization_barrier((total, rim, grad_query))
    total = scatter_sum(total, "cp")
    grad_cols = jnp.concatenate(
        [grad_in_cols[: length - 8], grad_in_cols[length - 8 :] + rim], axis=0
    )
    grad_keys = key_own + sum(p.astype(F32) for p in key_parts)
    back = jnp.concatenate(
        [grad_cols.astype(BF16), grad_query.astype(BF16), grad_keys.astype(BF16), grad_dt.astype(BF16)],
        axis=1,
    )
    back = to_groups(back.reshape(GROUPS, rows, DT_AT + 128))
    grad_x = back[:, :, 2 * NS : CW].transpose(1, 0, 2).reshape(rows, DS)
    grad_bc = jnp.sum(back[:, :, : 2 * NS].astype(F32), axis=0).astype(BF16)
    grad_q = back[:, :, Q_AT:KV_AT].transpose(1, 0, 2).reshape(rows, HEADS * HP)
    shared = back[:, :, KV_AT:DT_AT].astype(F32).reshape(KEY_HEADS, GROUPS // KEY_HEADS, rows, 2, HP)
    grad_kv = jnp.sum(shared, axis=1).transpose(1, 2, 0, 3).reshape(rows, 2 * KEY_HEADS * HP)
    grad_dt_tok = back[:, :, DT_AT : DT_AT + heads].transpose(1, 0, 2).reshape(rows, HM)
    grad_proj = jnp.concatenate(
        [
            grad_gate_pre.astype(BF16),
            grad_x,
            grad_bc,
            grad_dt_tok,
            grad_q,
            grad_kv.astype(BF16),
            jnp.zeros((rows, PROJ_WIDE - PROJ), BF16),
        ],
        axis=1,
    )
    tokens_back, grad_norm_in = in_back(
        times_halves_transposed(grad_proj[:, :PROJ], in_ours, in_theirs)
    )
    grad_tokens = grad_resid + tokens_back

    conv_full = jnp.concatenate(
        [
            lax.dynamic_update_slice_in_dim(
                jnp.zeros((KW, DS), F32), grad_taps[:KW, 2 * NS :], group * XW, 1
            ),
            grad_taps[:KW, : 2 * NS],
        ],
        axis=1,
    )
    head_full = lax.dynamic_update_slice_in_dim(
        jnp.zeros((3, HM), F32), grad_par[:3, :heads], group * heads, 1
    )
    parts = [
        a.reshape(-1) for a in (grad_norm_in, grad_norm_mid, grad_mamba_gain, conv_full, head_full)
    ]
    flat = jnp.concatenate(parts)
    flat = jnp.pad(flat, (0, 16 * 1024 - flat.shape[0])).reshape(16, 1024)
    total, flat = lax.optimization_barrier((total, flat))
    total = scatter_sum(total, "ux")
    grad_in, flat = sum_over_devices_call(normed_in, grad_proj, flat)
    grad_gu, grad_down, grad_mout, grad_aout = split_products(total[0], pairs, core)
    flat = flat.reshape(-1)
    small, at = [], 0
    for shape in ((1024,), (1024,), (DS,), (KW, DS + 2 * NS), (3, HM)):
        size = math.prod(shape)
        small.append(flat[at : at + size].reshape(shape))
        at += size
    return (
        layer_out,
        grad_tokens,
        small[0],
        small[1],
        small[2],
        small[3],
        small[4][0],
        small[4][1],
        small[4][2],
        grad_in[:, :PROJ],
        grad_mout,
        grad_aout,
        grad_gu,
        grad_down,
    )


def solution(mesh):
    fine = Mesh(mesh.devices.reshape(4, 4, 4, 2), TOKEN_AXES)
    by_token = P(TOKEN_AXES, None)
    by_row = P("fs", None)
    return jax.shard_map(
        shards,
        mesh=fine,
        in_specs=(by_token,) + (P(),) * 7 + (by_row,) * 5 + (by_token,),
        out_specs=(by_token, by_token) + (P(),) * 7 + (by_token,) * 5,
        check_vma=False,
    )
```

```python
import math

import jax
import jax.numpy as jnp
from jax import lax
from jax.experimental import pallas as pl
from jax.experimental.pallas import tpu as pltpu
from jax.sharding import Mesh
from jax.sharding import PartitionSpec as P

HP = 64
NS = 128
KW = 4
SBLK = 256
MASKED = -1e30
HIGHEST = lax.Precision.HIGHEST
F32 = jnp.float32
BF16 = jnp.bfloat16
VMEM_LIMIT = 56 * 1024 * 1024
XW = 192
CW = 448
HALO = 16
DT_AT = 640
Q_AT = 448
KV_AT = 512


def nn(a, b, precision=None):
    return lax.dot_general(
        a, b, (((1,), (0,)), ((), ())), precision=precision, preferred_element_type=F32
    )


def nt(a, b):
    return lax.dot_general(a, b, (((1,), (1,)), ((), ())), preferred_element_type=F32)


def tn(a, b):
    return lax.dot_general(a, b, (((0,), (0,)), ((), ())), preferred_element_type=F32)


def iota(shape, dim):
    return lax.broadcasted_iota(jnp.int32, shape, dim)


def spread(per_head, rows):
    return jnp.concatenate(
        [jnp.broadcast_to(per_head[:, h : h + 1], (rows, HP)) for h in range(XW // HP)], axis=1
    )


def head_sum_matrix():
    return (iota((XW, 128), 0) // HP == iota((XW, 128), 1)).astype(F32)


def conv_pre(ext, weights, base, lanes=slice(None)):
    pre = ext[pl.ds(base + HALO - 3, SBLK), :] * weights[0:1, :]
    for k in range(1, KW):
        pre = pre + ext[pl.ds(base + HALO - 3 + k, SBLK), :] * weights[k : k + 1, :]
    return pre


def step_and_log(slab, par_ref, base):
    raw = slab[pl.ds(base, SBLK), DT_AT:].astype(F32) + par_ref[1:2, :]
    step = jnp.maximum(raw, 0.0) + jnp.log1p(jnp.exp(-jnp.abs(raw)))
    return raw, step, -jnp.exp(par_ref[0:1, :]) * step


def ssd_forward(slab, halo, taps, par, y_out, state_out, c_out, cum_out, entry_out, ext):
    length = slab.shape[0]
    ext[pl.ds(0, HALO), :] = halo[...].astype(F32)
    ext[pl.ds(HALO, length), :] = slab[:, :CW].astype(F32)
    weights = taps[...]
    lower = iota((SBLK, SBLK), 0) >= iota((SBLK, SBLK), 1)
    tri = lower.astype(F32)
    state_out[...] = jnp.zeros_like(state_out)
    before = jnp.zeros((1, 128), F32)
    for k in range(length // SBLK):
        base = k * SBLK
        pre = conv_pre(ext, weights, base)
        conv = pre * jax.nn.sigmoid(pre)
        b_low = conv[:, :NS].astype(BF16)
        c_low = conv[:, NS : 2 * NS].astype(BF16)
        x = conv[:, 2 * NS :]
        raw, step, log = step_and_log(slab, par, base)
        cum = nn(tri, log, HIGHEST)
        cum_t = cum.T
        u = x * spread(step, SBLK)
        u_low = u.astype(BF16)
        inner = nt(c_low, b_low)
        state = state_out[pl.ds(0, XW), :]
        entry_out[k] = state
        parts = []
        for h in range(XW // HP):
            decay = jnp.exp(
                jnp.where(lower, cum[:, h : h + 1] - cum_t[h : h + 1, :], MASKED)
            )
            parts.append(nn((inner * decay).astype(BF16), u_low[:, h * HP : (h + 1) * HP]))
        carried = nt(c_low, state.astype(BF16)) * spread(jnp.exp(cum), SBLK)
        y_out[pl.ds(base, SBLK), :] = (
            jnp.concatenate(parts, axis=1) + carried + spread(par[2:3, :], 1) * x
        )
        last = cum[SBLK - 1 : SBLK, :]
        tail = (u * spread(jnp.exp(last - cum), SBLK)).astype(BF16)
        shrink = jnp.concatenate(
            [
                jnp.broadcast_to(jnp.exp(last[:, h : h + 1]), (HP, NS))
                for h in range(XW // HP)
            ],
            axis=0,
        )
        state_out[pl.ds(0, XW), :] = state * shrink + tn(tail, b_low)
        c_out[pl.ds(base, SBLK), :] = c_low
        cum_out[pl.ds(base, SBLK), :] = cum + before
        before = before + last
    state_out[pl.ds(XW, 8), :] = jnp.broadcast_to(before, (8, 128))


def ssd_forward_call(slab, halo, taps, par):
    length = slab.shape[0]
    return pl.pallas_call(
        ssd_forward,
        out_shape=(
            jax.ShapeDtypeStruct((length, XW), F32),
            jax.ShapeDtypeStruct((XW + 8, NS), F32),
            jax.ShapeDtypeStruct((length, NS), BF16),
            jax.ShapeDtypeStruct((length, 128), F32),
            jax.ShapeDtypeStruct((length // SBLK, XW, NS), F32),
        ),
        scratch_shapes=[pltpu.VMEM((length + HALO, CW), F32)],
        compiler_params=pltpu.CompilerParams(vmem_limit_bytes=VMEM_LIMIT),
        cost_estimate=pl.CostEstimate(
            flops=8_000_000_000, bytes_accessed=8_000_000, transcendentals=1_000_000
        ),
        name="ssd_forward",
    )(slab, halo, taps, par)


def shrink_rows(log_row):
    return jnp.concatenate(
        [jnp.broadcast_to(jnp.exp(log_row[:, h : h + 1]), (HP, NS)) for h in range(XW // HP)],
        axis=0,
    )


def ssd_join(y, c, cum, near, mid, far, attended, out, entering):
    state = near[pl.ds(0, XW), :] + shrink_rows(near[XW : XW + 1, :]) * (
        mid[pl.ds(0, XW), :] + shrink_rows(mid[XW : XW + 1, :]) * far[pl.ds(0, XW), :]
    )
    entering[...] = state
    state_low = state.astype(BF16)
    rows = y.shape[0]
    for base in range(0, rows, SBLK):
        at = pl.ds(base, SBLK)
        mixed = y[at, :] + nt(c[at, :], state_low) * spread(jnp.exp(cum[at, :]), SBLK)
        out[at, :] = jnp.concatenate([mixed, attended[at, :]], axis=1).astype(BF16)


def ssd_join_call(y, c, cum, near, mid, far, attended):
    return pl.pallas_call(
        ssd_join,
        out_shape=(
            jax.ShapeDtypeStruct((y.shape[0], XW + HP), BF16),
            jax.ShapeDtypeStruct((XW, NS), F32),
        ),
        compiler_params=pltpu.CompilerParams(vmem_limit_bytes=VMEM_LIMIT),
        name="ssd_join",
    )(y, c, cum, near, mid, far, attended)


def ssd_entry_gradient(grad, c, cum, out):
    rows = grad.shape[0]
    total = jnp.zeros((XW, NS), F32)
    for base in range(0, rows, SBLK):
        at = pl.ds(base, SBLK)
        scaled = grad[at, :XW].astype(F32) * spread(jnp.exp(cum[at, :]), SBLK)
        total = total + tn(scaled.astype(BF16), c[at, :])
    out[pl.ds(0, XW), :] = total
    out[pl.ds(XW, 8), :] = jnp.broadcast_to(cum[rows - 1 : rows, :], (8, 128))


def ssd_entry_gradient_call(grad, c, cum):
    return pl.pallas_call(
        ssd_entry_gradient,
        out_shape=jax.ShapeDtypeStruct((XW + 8, NS), F32),
        compiler_params=pltpu.CompilerParams(vmem_limit_bytes=VMEM_LIMIT),
        name="ssd_entry_gradient",
    )(grad, c, cum)


def ssd_backward(
    slab, halo, taps, par, grad, entry, cum_all, entering, near, mid, far,
    grad_in, grad_dt, grad_rim, grad_taps, grad_par, ext, gpre,
):
    length = slab.shape[0]
    chunks = length // SBLK
    ext[pl.ds(0, HALO), :] = halo[...].astype(F32)
    ext[pl.ds(HALO, length), :] = slab[:, :CW].astype(F32)
    gpre[pl.ds(length, HALO), :] = jnp.zeros((HALO, CW), F32)
    weights = taps[...]
    lower = iota((SBLK, SBLK), 0) >= iota((SBLK, SBLK), 1)
    tri = lower.astype(F32)
    upper = (iota((SBLK, SBLK), 0) <= iota((SBLK, SBLK), 1)).astype(F32)
    hsum = head_sum_matrix()
    rate = jnp.exp(par[0:1, :])
    skip = spread(par[2:3, :], 1)
    enter = entering[...]
    later = near[pl.ds(0, XW), :] + shrink_rows(near[XW : XW + 1, :]) * (
        mid[pl.ds(0, XW), :] + shrink_rows(mid[XW : XW + 1, :]) * far[pl.ds(0, XW), :]
    )
    g_decay = jnp.zeros((1, 128), F32)
    g_bias = jnp.zeros((1, 128), F32)
    g_skip = jnp.zeros((1, 128), F32)
    for k in reversed(range(chunks)):
        base = k * SBLK
        at = pl.ds(base, SBLK)
        pre = conv_pre(ext, weights, base)
        sig = jax.nn.sigmoid(pre)
        conv = pre * sig
        b_low = conv[:, :NS].astype(BF16)
        c_low = conv[:, NS : 2 * NS].astype(BF16)
        x = conv[:, 2 * NS :]
        raw, step, log = step_and_log(slab, par, base)
        cum = nn(tri, log, HIGHEST)
        cum_t = cum.T
        last = cum[SBLK - 1 : SBLK, :]
        step_wide = spread(step, SBLK)
        u_low = (x * step_wide).astype(BF16)
        u = u_low.astype(F32)
        gy_low = grad[at, :XW]
        gy = gy_low.astype(F32)
        if k:
            state = entry[k] + shrink_rows(cum_all[base - 1 : base, :]) * enter
        else:
            state = enter
        state_low = state.astype(BF16)
        later_low = later.astype(BF16)
        inner = nt(c_low, b_low)
        g_inner = jnp.zeros((SBLK, SBLK), F32)
        y_parts, gu_parts = [], []
        for h in range(XW // HP):
            lanes = slice(h * HP, (h + 1) * HP)
            decay = jnp.exp(
                jnp.where(lower, cum[:, h : h + 1] - cum_t[h : h + 1, :], MASKED)
            )
            kernel = (inner * decay).astype(BF16)
            y_parts.append(nn(kernel, u_low[:, lanes]))
            gu_parts.append(tn(kernel, gy_low[:, lanes]))
            g_inner = g_inner + nt(gy_low[:, lanes], u_low[:, lanes]) * decay
        g_inner_low = g_inner.astype(BF16)
        enter_wide = spread(jnp.exp(cum), SBLK)
        tail_wide = spread(jnp.exp(last - cum), SBLK)
        gy_scaled = (gy * enter_wide).astype(BF16)
        u_scaled = (u * tail_wide).astype(BF16)
        y = jnp.concatenate(y_parts, axis=1) + nt(c_low, state_low) * enter_wide
        tail = nt(b_low, later_low) * tail_wide
        gu = jnp.concatenate(gu_parts, axis=1) + tail
        gc = nn(g_inner_low, b_low) + nn(gy_scaled, state_low)
        gb = tn(g_inner_low, c_low) + nn(u_scaled, later_low)
        shrink = shrink_rows(last)
        both = nn(gy * y - u * gu, hsum, HIGHEST)
        tail_sum = jnp.sum(nn(u * tail, hsum, HIGHEST), axis=0, keepdims=True)
        across = jnp.sum(
            jnp.sum(later * state * shrink, axis=1, keepdims=True) * hsum, axis=0, keepdims=True
        )
        g_log = nn(upper, both, HIGHEST) + tail_sum + across
        g_step = nn(x * gu, hsum, HIGHEST) - rate * g_log
        g_raw = g_step * jax.nn.sigmoid(raw)
        g_decay = g_decay + jnp.sum(g_log * log, axis=0, keepdims=True)
        g_bias = g_bias + jnp.sum(g_raw, axis=0, keepdims=True)
        g_skip = g_skip + jnp.sum(nn(gy * x, hsum, HIGHEST), axis=0, keepdims=True)
        grad_dt[at, :] = g_raw
        g_conv = jnp.concatenate([gb, gc, step_wide * gu + skip * gy], axis=1)
        gpre[at, :] = g_conv * (sig + conv * (1.0 - sig))
        later = shrink * later + tn(gy_scaled, c_low)
    for k in range(chunks):
        base = k * SBLK
        acc = gpre[pl.ds(base + 3, SBLK), :] * weights[0:1, :]
        for tap in range(1, KW):
            acc = acc + gpre[pl.ds(base + 3 - tap, SBLK), :] * weights[tap : tap + 1, :]
        grad_in[pl.ds(base, SBLK), :] = acc
    first = gpre[pl.ds(0, 8), :]
    rim = jnp.zeros((8, CW), F32)
    rows = iota((8, CW), 0)
    for back in range(1, KW):
        term = jnp.zeros((1, CW), F32)
        for tap in range(KW):
            t = 3 - tap - back
            if 0 <= t:
                term = term + first[t : t + 1, :] * weights[tap : tap + 1, :]
        rim = jnp.where(rows == 8 - back, term, rim)
    grad_rim[...] = rim
    g_taps = jnp.zeros((8, CW), F32)
    rows = iota((8, CW), 0)
    for tap in range(KW):
        total = jnp.zeros((1, CW), F32)
        for k in range(chunks):
            base = k * SBLK
            total = total + jnp.sum(
                gpre[pl.ds(base, SBLK), :] * ext[pl.ds(base + HALO - 3 + tap, SBLK), :],
                axis=0,
                keepdims=True,
            )
        g_taps = jnp.where(rows == tap, total, g_taps)
    grad_taps[...] = g_taps
    rows = iota((8, 128), 0)
    grad_par[...] = jnp.where(
        rows == 0, g_decay, jnp.where(rows == 1, g_bias, jnp.where(rows == 2, g_skip, 0.0))
    )


def ssd_backward_call(slab, halo, taps, par, grad, entry, cum, entering, near, mid, far):
    length = slab.shape[0]
    return pl.pallas_call(
        ssd_backward,
        out_shape=(
            jax.ShapeDtypeStruct((length, CW), F32),
            jax.ShapeDtypeStruct((length, 128), F32),
            jax.ShapeDtypeStruct((8, CW), F32),
            jax.ShapeDtypeStruct((8, CW), F32),
            jax.ShapeDtypeStruct((8, 128), F32),
        ),
        scratch_shapes=[
            pltpu.VMEM((length + HALO, CW), F32),
            pltpu.VMEM((length + HALO, CW), F32),
        ],
        compiler_params=pltpu.CompilerParams(vmem_limit_bytes=VMEM_LIMIT),
        cost_estimate=pl.CostEstimate(
            flops=20_000_000_000, bytes_accessed=12_000_000, transcendentals=2_000_000
        ),
        name="ssd_backward",
    )(slab, halo, taps, par, grad, entry, cum, entering, near, mid, far)


QB = 256
KB = 512


def place_keys(rank, parts, kv):
    length = parts[0].shape[0]
    for back, part in enumerate(parts):

        @pl.when(rank >= back)
        def _():
            kv[pl.ds(pl.multiple_of((rank - back) * length, length), length), :] = part[...]


def attend_forward(rank_ref, slab, near, mid, far, out, lse, kv, own):
    length = slab.shape[0]
    rank = rank_ref[0]
    offset = rank * length
    scale = HP**-0.5
    ahead = iota((QB, KB), 0) - iota((QB, KB), 1)
    own[...] = slab[:, KV_AT:DT_AT]
    place_keys(rank, (own, near, mid, far), kv)

    def q_step(i, _):
        at = pl.ds(pl.multiple_of(i * QB, QB), QB)
        q_blk = (slab[at, Q_AT:KV_AT].astype(F32) * scale).astype(BF16)
        first = offset + i * QB

        def block(j, carry, masked):
            top, total, acc = carry
            at = pl.ds(pl.multiple_of(j * KB, KB), KB)
            s = nt(q_blk, kv[at, :HP])
            if masked:
                s = jnp.where(ahead >= j * KB - first, s, MASKED)
            new = jnp.maximum(top, jnp.max(s, axis=1, keepdims=True))
            p = jnp.exp(s - new)
            fade = jnp.exp(top - new)
            total = total * fade + jnp.sum(p, axis=1, keepdims=True)
            acc = acc * fade + nn(p.astype(BF16), kv[at, HP:])
            return new, total, acc

        whole = first // KB
        carry = (
            jnp.full((QB, 1), MASKED, F32),
            jnp.zeros((QB, 1), F32),
            jnp.zeros((QB, HP), F32),
        )
        carry = lax.fori_loop(0, whole, lambda j, c: block(j, c, False), carry)
        top, total, acc = block(whole, carry, True)
        out[at, :] = acc / total
        lse[at, :] = jnp.broadcast_to(top + jnp.log(total), (QB, 128))
        return 0

    lax.fori_loop(0, length // QB, q_step, 0)


def attend_forward_call(rank, slab, near, mid, far):
    length = slab.shape[0]
    vm = pl.BlockSpec(memory_space=pltpu.VMEM)
    return pl.pallas_call(
        attend_forward,
        in_specs=[pl.BlockSpec(memory_space=pltpu.SMEM)] + [vm] * 4,
        out_shape=(
            jax.ShapeDtypeStruct((length, HP), F32),
            jax.ShapeDtypeStruct((length, 128), F32),
        ),
        scratch_shapes=[
            pltpu.VMEM((4 * length, 2 * HP), BF16),
            pltpu.VMEM((length, 2 * HP), BF16),
        ],
        compiler_params=pltpu.CompilerParams(vmem_limit_bytes=VMEM_LIMIT),
        cost_estimate=pl.CostEstimate(
            flops=8_000_000_000, bytes_accessed=4_000_000, transcendentals=4_000_000
        ),
        name="attend_forward",
    )(rank, slab, near, mid, far)


def attend_backward(
    rank_ref, slab, near, mid, far, g, out, lse, gq, g_own, g_near, g_mid, g_far, kv, own, acc
):
    length = slab.shape[0]
    rank = rank_ref[0]
    offset = rank * length
    scale = HP**-0.5
    ahead = iota((QB, KB), 0) - iota((QB, KB), 1)
    own[...] = slab[:, KV_AT:DT_AT]
    place_keys(rank, (own, near, mid, far), kv)
    acc[...] = jnp.zeros_like(acc)

    def q_step(i, _):
        at_q = pl.ds(pl.multiple_of(i * QB, QB), QB)
        q_blk = (slab[at_q, Q_AT:KV_AT].astype(F32) * scale).astype(BF16)
        g_low = g[at_q, XW:]
        delta = jnp.sum(g_low.astype(F32) * out[at_q, :], axis=1, keepdims=True)
        log_total = lse[at_q, 0:1]
        first = offset + i * QB

        def block(j, gq_acc, masked):
            at = pl.ds(pl.multiple_of(j * KB, KB), KB)
            k_blk = kv[at, :HP]
            s = nt(q_blk, k_blk)
            if masked:
                s = jnp.where(ahead >= j * KB - first, s, MASKED)
            p = jnp.exp(s - log_total)
            dp = nt(g_low, kv[at, HP:])
            ds = (p * (dp - delta)).astype(BF16)
            acc[at, :] += jnp.concatenate([tn(ds, q_blk), tn(p.astype(BF16), g_low)], axis=1)
            return gq_acc + nn(ds, k_blk)

        whole = first // KB
        carry = jnp.zeros((QB, HP), F32)
        carry = lax.fori_loop(0, whole, lambda j, c: block(j, c, False), carry)
        gq[at_q, :] = block(whole, carry, True) * scale
        return 0

    lax.fori_loop(0, length // QB, q_step, 0)
    for back, target in enumerate((g_own, g_near, g_mid, g_far)):

        @pl.when(rank >= back)
        def _():
            at = pl.ds(pl.multiple_of((rank - back) * length, length), length)
            target[...] = acc[at, :].astype(target.dtype)

        @pl.when(rank < back)
        def _():
            target[...] = jnp.zeros_like(target)


def attend_backward_call(rank, slab, near, mid, far, g, out, lse):
    length = slab.shape[0]
    vm = pl.BlockSpec(memory_space=pltpu.VMEM)
    keys = jax.ShapeDtypeStruct((length, 2 * HP), BF16)
    return pl.pallas_call(
        attend_backward,
        in_specs=[pl.BlockSpec(memory_space=pltpu.SMEM)] + [vm] * 7,
        out_shape=(
            jax.ShapeDtypeStruct((length, HP), F32),
            jax.ShapeDtypeStruct((length, 2 * HP), F32),
            keys,
            keys,
            keys,
        ),
        scratch_shapes=[
            pltpu.VMEM((4 * length, 2 * HP), BF16),
            pltpu.VMEM((length, 2 * HP), BF16),
            pltpu.VMEM((4 * length, 2 * HP), F32),
        ],
        compiler_params=pltpu.CompilerParams(vmem_limit_bytes=VMEM_LIMIT),
        cost_estimate=pl.CostEstimate(
            flops=20_000_000_000, bytes_accessed=4_000_000, transcendentals=4_000_000
        ),
        name="attend_backward",
    )(rank, slab, near, mid, far, g, out, lse)


CORE_ROWS = 16
PARTS = (0, 768, 1536, 2176)
ORDERS = ((0, 1, 2), (1, 2, 0), (2, 0, 1))
TORUS = ("fs", "cp", "ux")


def sum_over_devices(
    left, right, small, out, small_out,
    left_in, right_in, part0, part1, part2, got10, got11, got12, mid0, mid1, mid2,
    got20, got21, got22, end0, end1, end2, got30, got31, got32, done, done_in, small_in, small_core,
    core_send, core_recv, send, recv, small_send, small_recv,
):
    mesh_kind = pl.DeviceIdType.MESH
    core = lax.axis_index("uc")
    place = [lax.axis_index(a) for a in TORUS]
    other = {"uc": 1 - core}
    half = right.shape[1] // 2
    rows = left.shape[0]

    def peer(axis, shift):
        return {TORUS[axis]: lax.rem(place[axis] + shift, 4)}

    barrier = pltpu.get_barrier_semaphore()
    pl.semaphore_signal(barrier, inc=1, device_id=other, device_id_type=mesh_kind)
    for axis in range(3):
        for shift in (1, 2, 3):
            pl.semaphore_signal(
                barrier, inc=1, device_id=peer(axis, shift), device_id_type=mesh_kind
            )
    pl.semaphore_wait(barrier, 10)

    def remote(src, dst, send_sem, recv_sem, target):
        copy = pltpu.make_async_remote_copy(
            src_ref=src, dst_ref=dst, send_sem=send_sem, recv_sem=recv_sem,
            device_id=target, device_id_type=mesh_kind,
        )
        copy.start()
        return copy

    theirs = pl.ds(pl.multiple_of((1 - core) * half, 128), half)
    ours = pl.ds(pl.multiple_of(core * half, 128), half)
    core_copies = [
        remote(left, left_in, core_send.at[0], core_recv.at[0], other),
        remote(right.at[:, theirs], right_in, core_send.at[1], core_recv.at[1], other),
        remote(small, small_core, core_send.at[2], core_recv.at[2], other),
    ]
    for copy in core_copies:
        copy.wait()

    parts = (part0, part1, part2)
    got1, got2, got3 = (got10, got11, got12), (got20, got21, got22), (got30, got31, got32)
    mids, ends = (mid0, mid1, mid2), (end0, end1, end2)
    lefts = [(left[:, f * 256 : (f + 1) * 256], left_in[:, f * 256 : (f + 1) * 256]) for f in range(4)]
    first = []
    for p in range(3):
        width = PARTS[p + 1] - PARTS[p]
        at = pl.ds(pl.multiple_of(core * half + PARTS[p], 128), width)
        mine, their = right[:, at], right_in[:, PARTS[p] : PARTS[p + 1]]
        rights = jnp.concatenate([mine, their], axis=0)
        for f in range(4):
            block = tn(jnp.concatenate(lefts[f], axis=0), rights).astype(BF16)
            for c in range(4):
                for x in range(4):
                    where = (f, c, x)
                    a0, a1, a2 = (where[a] for a in ORDERS[p])
                    start = (c * 4 + x) * CORE_ROWS
                    parts[p][a0, a1, a2] = block[start : start + CORE_ROWS]
        axis = ORDERS[p][0]
        first.append(
            [
                remote(
                    parts[p].at[lax.rem(place[axis] + shift, 4)], got1[p].at[shift - 1],
                    send.at[p, 0, shift - 1], recv.at[p, 0, shift - 1], peer(axis, shift),
                )
                for shift in (1, 2, 3)
            ]
        )

    total = small[...] + small_core[...]
    for axis in range(3):
        small_in[axis, place[axis]] = total
        copies = [
            remote(
                small_in.at[axis, place[axis]], small_in.at[axis, place[axis]],
                small_send.at[axis, shift - 1], small_recv.at[axis, shift - 1], peer(axis, shift),
            )
            for shift in (1, 2, 3)
        ]
        for copy in copies:
            copy.wait()
        total = (small_in[axis, 0] + small_in[axis, 1]) + (small_in[axis, 2] + small_in[axis, 3])
    small_out[...] = total

    def add(source, slots, index):
        acc = source[index].astype(F32)
        for s in range(3):
            acc = acc + slots[s].astype(F32)
        return acc

    second = []
    for p in range(3):
        for copy in first[p]:
            copy.wait()
        for i in range(4):
            acc = parts[p][place[ORDERS[p][0]], i].astype(F32)
            for s in range(3):
                acc = acc + got1[p][s, i].astype(F32)
            mids[p][i] = acc.astype(BF16)
        axis = ORDERS[p][1]
        second.append(
            [
                remote(
                    mids[p].at[lax.rem(place[axis] + shift, 4)], got2[p].at[shift - 1],
                    send.at[p, 1, shift - 1], recv.at[p, 1, shift - 1], peer(axis, shift),
                )
                for shift in (1, 2, 3)
            ]
        )
    third = []
    for p in range(3):
        for copy in second[p]:
            copy.wait()
        ends[p][...] = add(mids[p], got2[p], place[ORDERS[p][1]]).astype(BF16)
        axis = ORDERS[p][2]
        third.append(
            [
                remote(
                    ends[p].at[lax.rem(place[axis] + shift, 4)], got3[p].at[shift - 1],
                    send.at[p, 2, shift - 1], recv.at[p, 2, shift - 1], peer(axis, shift),
                )
                for shift in (1, 2, 3)
            ]
        )
    for p in range(3):
        for copy in third[p]:
            copy.wait()
        done[:, PARTS[p] : PARTS[p + 1]] = add(ends[p], got3[p], place[ORDERS[p][2]])
    keep = pl.ds(pl.multiple_of(core * 8, 8), 8)
    give = pl.ds(pl.multiple_of((1 - core) * 8, 8), 8)
    last = remote(done.at[give, :], done_in, core_send.at[3], core_recv.at[3], other)
    out[:, ours] = done[keep, :]
    last.wait()
    out[:, theirs] = done_in[...]


def sum_over_devices_call(left, right, small):
    half = right.shape[1] // 2
    widths = [PARTS[p + 1] - PARTS[p] for p in range(3)]

    def blocks(*lead):
        return [pltpu.VMEM(lead + (CORE_ROWS, w), BF16) for w in widths]

    return pl.pallas_call(
        sum_over_devices,
        in_specs=[pl.BlockSpec(memory_space=pltpu.VMEM)] * 3,
        out_specs=[pl.BlockSpec(memory_space=pltpu.VMEM)] * 2,
        out_shape=(
            jax.ShapeDtypeStruct((8, 2 * half), F32),
            jax.ShapeDtypeStruct(small.shape, F32),
        ),
        scratch_shapes=[
            pltpu.VMEM(left.shape, BF16),
            pltpu.VMEM((left.shape[0], half), BF16),
            *blocks(4, 4, 4),
            *blocks(3, 4, 4),
            *blocks(4, 4),
            *blocks(3, 4),
            *blocks(4),
            *blocks(3),
            pltpu.VMEM((CORE_ROWS, half), F32),
            pltpu.VMEM((8, half), F32),
            pltpu.VMEM((3, 4) + small.shape, F32),
            pltpu.VMEM(small.shape, F32),
            pltpu.SemaphoreType.DMA((4,)),
            pltpu.SemaphoreType.DMA((4,)),
            pltpu.SemaphoreType.DMA((3, 3, 3)),
            pltpu.SemaphoreType.DMA((3, 3, 3)),
            pltpu.SemaphoreType.DMA((3, 3)),
            pltpu.SemaphoreType.DMA((3, 3)),
        ],
        compiler_params=pltpu.CompilerParams(
            vmem_limit_bytes=VMEM_LIMIT, collective_id=0, has_side_effects=True
        ),
        cost_estimate=pl.CostEstimate(
            flops=1_200_000_000, bytes_accessed=4_000_000, transcendentals=0
        ),
        name="sum_over_devices",
    )(left, right, small)


HM = 24
GROUPS = 8
HEADS = 8
KEY_HEADS = 2
FF = 2048
DS = 1536
PROJ = 4120
PROJ_WIDE = 4352
EPSILON = 1e-05
TOKEN_AXES = ("fs", "cp", "ux", "uc")


def rms_norm(values, norm_gain):
    return (
        values * lax.rsqrt(jnp.mean(values * values, axis=-1, keepdims=True) + EPSILON) * norm_gain
    )


def gated_norm(mixed_heads, gate_pre, norm_gain):
    return rms_norm(mixed_heads * jax.nn.silu(gate_pre), norm_gain)


def from_behind(block, distance):
    return lax.ppermute(block, "cp", [(i - distance, i) for i in range(distance, 4)])


def from_ahead(block, distance):
    return lax.ppermute(block, "cp", [(i, i - distance) for i in range(distance, 4)])


def other_core(block):
    return lax.ppermute(block, "uc", [(0, 1), (1, 0)])


def columns_half(block, half):
    width = block.shape[1] // 2
    return lax.dynamic_slice_in_dim(block, half * width, width, 1)


def gather_half(shard, core):
    rows = shard.shape[0] // 2
    mine = lax.dynamic_slice_in_dim(shard, core * rows, rows, 0)
    return lax.all_gather(mine, "fs", axis=0, tiled=True)


def gather_by_permutes(shard):
    got = jnp.stack(
        [shard]
        + [lax.ppermute(shard, "fs", [(i, (i + s) % 4) for i in range(4)]) for s in (1, 2, 3)]
    )
    order = jnp.mod(lax.axis_index("fs") - jnp.arange(4), 4)
    return jnp.take(got, order, axis=0).reshape(-1, shard.shape[1])


def both_cores(left, right, core):
    lefts = jnp.concatenate([left, other_core(left)], axis=0)
    rights = jnp.concatenate(
        [columns_half(right, core), other_core(columns_half(right, 1 - core))], axis=0
    )
    return lefts, rights


def core_halves(rows, core):
    r = rows.shape[0] // 2
    mine = lax.dynamic_slice_in_dim(rows, core * r, r, 0)
    theirs = other_core(lax.dynamic_slice_in_dim(rows, (1 - core) * r, r, 0))
    return jnp.concatenate(
        [jnp.where(core == 0, mine, theirs), jnp.where(core == 0, theirs, mine)], axis=1
    ).astype(F32)


def weight_products(pairs, core):
    blocks = []
    for left, right in pairs:
        lefts, rights = both_cores(left, right, core)
        for at in range(0, rights.shape[1], 512):
            part = tn(lefts, rights[:, at : at + 512]).astype(BF16)
            blocks.append(part.reshape(64, part.shape[0] // 64, 512))
    return jnp.concatenate(blocks, axis=1)


def split_products(total, pairs, core):
    results, at = [], 0
    for left, right in pairs:
        r = left.shape[1] // 64
        count = right.shape[1] // 1024
        whole = jnp.concatenate(
            [total[at + i * r : at + (i + 1) * r] for i in range(count)], axis=1
        )
        at += count * r
        results.append(core_halves(whole, core))
    return results


def scatter_sum(total, axis):
    return lax.psum_scatter(total, axis, scatter_dimension=0, tiled=True)


def shards(
    tokens,
    norm_in,
    norm_mid,
    mamba_gain,
    conv_weight,
    decay_log,
    dt_bias,
    skip_gain,
    w_in,
    w_mout,
    w_aout,
    w_gu,
    w_down,
    grad_out,
):
    part_rank = lax.axis_index("cp")
    core = lax.axis_index("uc")
    group = lax.axis_index("ux") * 2 + core
    rows = tokens.shape[0]
    length = GROUPS * rows
    heads = HM // GROUPS
    in_ours = gather_half(w_in, core)
    in_theirs = other_core(in_ours)
    mout_ours = gather_half(w_mout, core)
    full_aout = gather_by_permutes(w_aout)
    gu_ours = gather_half(w_gu, core)
    down_ours = gather_half(w_down, core)

    def halves(block):
        pieces = block.reshape(rows, 4, 2, block.shape[1] // 8)
        picked = [
            lax.dynamic_index_in_dim(pieces, which, 2, False).reshape(rows, block.shape[1] // 2)
            for which in (core, 1 - core)
        ]
        return picked

    def times_halves(block, ours, theirs):
        own, rest = halves(block)
        return nn(own, ours) + nn(rest, theirs)

    def times_halves_transposed(block, ours, theirs):
        own = nt(block, ours).reshape(rows, 4, -1)
        rest = nt(block, theirs).reshape(rows, 4, -1)
        pieces = jnp.where(core == 0, jnp.stack([own, rest], 2), jnp.stack([rest, own], 2))
        return pieces.reshape(rows, -1)

    def to_groups(blocks):
        return lax.all_to_all(blocks, ("ux", "uc"), split_axis=0, concat_axis=0, tiled=True)

    resid_in = tokens.astype(F32)
    normed_f, in_back = jax.vjp(rms_norm, resid_in, norm_in)
    normed_in = normed_f.astype(BF16)
    normed_in, full_aout = lax.optimization_barrier((normed_in, full_aout))
    projected = times_halves(normed_in, in_ours, in_theirs)
    gate_pre = projected[:, :DS]
    low = projected[:, DS:].astype(BF16)
    q_at = DS + 2 * NS + HM
    k_at = q_at + HEADS * HP
    v_at = k_at + KEY_HEADS * HP
    blocks = []
    for g in range(GROUPS):
        key = g * KEY_HEADS // GROUPS
        blocks.append(
            jnp.concatenate(
                [
                    low[:, DS : DS + 2 * NS],
                    low[:, g * XW : (g + 1) * XW],
                    low[:, q_at + g * HP : q_at + (g + 1) * HP],
                    low[:, k_at + key * HP : k_at + (key + 1) * HP],
                    low[:, v_at + key * HP : v_at + (key + 1) * HP],
                    low[:, DS + 2 * NS + g * heads : DS + 2 * NS + (g + 1) * heads],
                    jnp.zeros((rows, 128 - heads), BF16),
                ],
                axis=1,
            )
        )
    slab = to_groups(jnp.stack(blocks)).reshape(length, DT_AT + 128)

    taps = jnp.concatenate(
        [conv_weight[:, DS:], lax.dynamic_slice_in_dim(conv_weight, group * XW, XW, 1)], axis=1
    )
    taps = jnp.pad(taps, ((0, 8 - KW), (0, 0)))
    per_head = jnp.stack([decay_log, dt_bias, skip_gain])
    par = jnp.pad(
        lax.dynamic_slice_in_dim(per_head, group * heads, heads, 1), ((0, 5), (0, 128 - heads))
    )
    rank = part_rank.astype(jnp.int32).reshape(1)

    halo = from_behind(slab[length - HALO :, :CW], 1)
    own_keys = slab[:, KV_AT:DT_AT]
    keys = [from_behind(own_keys, d) for d in (1, 2, 3)]
    y, state, c_low, cum, entry = ssd_forward_call(slab, halo, taps, par)
    mout_ours, y = lax.optimization_barrier((mout_ours, y))
    mout_theirs = other_core(mout_ours)
    states = [from_behind(state, d) for d in (1, 2, 3)]
    attended, lse = attend_forward_call(rank, slab, *keys)
    gu_ours, attended = lax.optimization_barrier((gu_ours, attended))
    gu_theirs = other_core(gu_ours)
    joined, entering = ssd_join_call(y, c_low, cum, *states, attended)
    tok = to_groups(joined.reshape(GROUPS, rows, XW + HP)).transpose(1, 0, 2)
    down_ours, tok = lax.optimization_barrier((down_ours, tok))
    down_theirs = other_core(down_ours)
    mixed_tok = tok[:, :, :XW].reshape(rows, DS)
    attended_tok = tok[:, :, XW:].reshape(rows, HEADS * HP)

    branch_f, gate_back = jax.vjp(gated_norm, mixed_tok.astype(F32), gate_pre, mamba_gain)
    branch_low = branch_f.astype(BF16)
    resid_mid = resid_in + times_halves(branch_low, mout_ours, mout_theirs) + nn(attended_tok, full_aout)
    normed_mid_f, mid_back = jax.vjp(rms_norm, resid_mid, norm_mid)
    normed_mid = normed_mid_f.astype(BF16)
    gate_up = times_halves(normed_mid, gu_ours, gu_theirs)
    gate_half = gate_up[:, :FF]
    up_half = gate_up[:, FF:]
    sigmoid_gate = jax.nn.sigmoid(gate_half)
    hidden = (gate_half * sigmoid_gate * up_half).astype(BF16)
    layer_out = (resid_mid + times_halves(hidden, down_ours, down_theirs)).astype(BF16)
    grad_hidden = times_halves_transposed(grad_out, down_ours, down_theirs)
    grad_gate = grad_hidden * up_half * sigmoid_gate * (1.0 + gate_half * (1.0 - sigmoid_gate))
    grad_up = grad_hidden * gate_half * sigmoid_gate
    grad_gate_up = jnp.concatenate([grad_gate, grad_up], axis=1).astype(BF16)
    resid_back, grad_norm_mid = mid_back(
        times_halves_transposed(grad_gate_up, gu_ours, gu_theirs)
    )
    grad_resid = grad_out.astype(F32) + resid_back
    resid_low = grad_resid.astype(BF16)
    grad_mixed, grad_gate_pre, grad_mamba_gain = gate_back(
        times_halves_transposed(resid_low, mout_ours, mout_theirs)
    )
    grad_attended = nt(resid_low, full_aout)
    grad_blocks = jnp.concatenate(
        [
            grad_mixed.astype(BF16).reshape(rows, GROUPS, XW),
            grad_attended.astype(BF16).reshape(rows, GROUPS, HP),
        ],
        axis=2,
    ).transpose(1, 0, 2)
    grad = to_groups(grad_blocks).reshape(length, XW + HP)
    pairs = [
        (normed_mid, grad_gate_up),
        (hidden, grad_out),
        (branch_low, resid_low),
        (attended_tok, resid_low),
    ]
    total = scatter_sum(weight_products(pairs, core), "fs")

    entry_gradient = ssd_entry_gradient_call(grad, c_low, cum)
    later = [from_ahead(entry_gradient, d) for d in (1, 2, 3)]
    grad_query, key_own, *key_parts = attend_backward_call(rank, slab, *keys, grad, attended, lse)
    key_parts = [from_ahead(p, d + 1) for d, p in enumerate(key_parts)]
    grad_in_cols, grad_dt, rim, grad_taps, grad_par = ssd_backward_call(
        slab, halo, taps, par, grad, entry, cum, entering, *later
    )
    rim = from_ahead(rim, 1)
    total, rim, grad_query = lax.optimization_barrier((total, rim, grad_query))
    total = scatter_sum(total, "cp")
    grad_cols = jnp.concatenate(
        [grad_in_cols[: length - 8], grad_in_cols[length - 8 :] + rim], axis=0
    )
    grad_keys = key_own + sum(p.astype(F32) for p in key_parts)
    back = jnp.concatenate(
        [grad_cols.astype(BF16), grad_query.astype(BF16), grad_keys.astype(BF16), grad_dt.astype(BF16)],
        axis=1,
    )
    back = to_groups(back.reshape(GROUPS, rows, DT_AT + 128))
    grad_x = back[:, :, 2 * NS : CW].transpose(1, 0, 2).reshape(rows, DS)
    grad_bc = jnp.sum(back[:, :, : 2 * NS].astype(F32), axis=0).astype(BF16)
    grad_q = back[:, :, Q_AT:KV_AT].transpose(1, 0, 2).reshape(rows, HEADS * HP)
    shared = back[:, :, KV_AT:DT_AT].astype(F32).reshape(KEY_HEADS, GROUPS // KEY_HEADS, rows, 2, HP)
    grad_kv = jnp.sum(shared, axis=1).transpose(1, 2, 0, 3).reshape(rows, 2 * KEY_HEADS * HP)
    grad_dt_tok = back[:, :, DT_AT : DT_AT + heads].transpose(1, 0, 2).reshape(rows, HM)
    grad_proj = jnp.concatenate(
        [
            grad_gate_pre.astype(BF16),
            grad_x,
            grad_bc,
            grad_dt_tok,
            grad_q,
            grad_kv.astype(BF16),
            jnp.zeros((rows, PROJ_WIDE - PROJ), BF16),
        ],
        axis=1,
    )
    tokens_back, grad_norm_in = in_back(
        times_halves_transposed(grad_proj[:, :PROJ], in_ours, in_theirs)
    )
    grad_tokens = grad_resid + tokens_back

    conv_full = jnp.concatenate(
        [
            lax.dynamic_update_slice_in_dim(
                jnp.zeros((KW, DS), F32), grad_taps[:KW, 2 * NS :], group * XW, 1
            ),
            grad_taps[:KW, : 2 * NS],
        ],
        axis=1,
    )
    head_full = lax.dynamic_update_slice_in_dim(
        jnp.zeros((3, HM), F32), grad_par[:3, :heads], group * heads, 1
    )
    parts = [
        a.reshape(-1) for a in (grad_norm_in, grad_norm_mid, grad_mamba_gain, conv_full, head_full)
    ]
    flat = jnp.concatenate(parts)
    flat = jnp.pad(flat, (0, 16 * 1024 - flat.shape[0])).reshape(16, 1024)
    total, flat = lax.optimization_barrier((total, flat))
    total = scatter_sum(total, "ux")
    grad_in, flat = sum_over_devices_call(normed_in, grad_proj, flat)
    grad_gu, grad_down, grad_mout, grad_aout = split_products(total[0], pairs, core)
    flat = flat.reshape(-1)
    small, at = [], 0
    for shape in ((1024,), (1024,), (DS,), (KW, DS + 2 * NS), (3, HM)):
        size = math.prod(shape)
        small.append(flat[at : at + size].reshape(shape))
        at += size
    return (
        layer_out,
        grad_tokens,
        small[0],
        small[1],
        small[2],
        small[3],
        small[4][0],
        small[4][1],
        small[4][2],
        grad_in[:, :PROJ],
        grad_mout,
        grad_aout,
        grad_gu,
        grad_down,
    )


def solution(mesh):
    fine = Mesh(mesh.devices.reshape(4, 4, 4, 2), TOKEN_AXES)
    by_token = P(TOKEN_AXES, None)
    by_row = P("fs", None)
    return jax.shard_map(
        shards,
        mesh=fine,
        in_specs=(by_token,) + (P(),) * 7 + (by_row,) * 5 + (by_token,),
        out_specs=(by_token, by_token) + (P(),) * 7 + (by_token,) * 5,
        check_vma=False,
    )
```
